32 devices in a mesh: groups: 2 (over x), adapter: 4 (over y, core), dp: 4 (over z).
Axes of the slice: x: 2, y: 2, z: 4, core: 2. Of those that a mesh axis runs over, the one named last changes fastest.
Arguments:
- acts: bfloat16 [16384, 8192], P(('groups', 'dp'), 'adapter'), parts along dimension 0, may hold values from -6 to 6
- out_grad: bfloat16 [16384, 2048], P(('groups', 'dp'), 'adapter'), parts along dimension 0, may hold values from -1.5 to 1.5
- tenant_ids: int32 [128, 1], P(('groups', 'dp')), parts along dimension 0, may hold values from 0 to 3
- slot_map: int32 [8], P('groups'), parts along dimension 0, may hold values from 0 to 3, each once
- down_pool: bfloat16 [8, 8192, 128], P(('groups', 'adapter')), parts along dimension 0, may hold values from -0.0625 to 0.0625
- up_pool: bfloat16 [8, 64, 2048], P(('groups', 'adapter')), parts along dimension 0, may hold values from -0.75 to 0.75
Outputs:
- acts_grad: bfloat16 [16384, 8192], P(('groups', 'dp'), 'adapter'), parts along dimension 0
- down_grad: bfloat16 [8, 8192, 128], P(('groups', 'adapter')), parts along dimension 0
- up_grad: bfloat16 [8, 64, 2048], P(('groups', 'adapter')), parts along dimension 0
The draws below stay inside these ranges and needn't reach their ends.
There are 2 independent parts, one for each index of `groups`. The reference program is written for one: setup_inputs(seed, part) draws one part's arguments, and reference() takes and returns one part's arrays. A program takes and returns all parts, laid end to end along the dimension named above; each array names one. Nothing has to cross between parts.
Inputs may be any that keep to these rules, and one draw needn't show every extreme that they name: `tenant_ids`: every tenant owns at least one block. `slot_map`: each pool row belongs to exactly one tenant.
All inputs are finite; a program needn't handle non-finite values.
Results may differ from the reference program's by a relative error of at most 0.0052.
Values may be sent and summed in bfloat16 or wider, within the bound.
No kernel may reach another device: no remote copies, remote signals or barrier semaphores. Data moves between devices by JAX's collectives and lax.ppermute only.
A program may use at most 192 MiB of HBM per device.

```python
import jax
import jax.numpy as jnp
from jax import lax

D = 8192
DKV = 1024
R = 64
BLOCK = 128
BLOCKS = 64
TOKENS = 8192
TENANTS = 4


def level_of(stream_key, shape, pieces, low, top_value):
    level = 1.0
    for dim, parts in pieces:
        heights = jax.random.uniform(jax.random.fold_in(jax.random.fold_in(stream_key, 6), dim), (parts,), jnp.float32, low / len(pieces), top_value / len(pieces))
        level = level * jnp.repeat(jnp.exp(heights), shape[dim] // parts).reshape((-1,) + (1,) * (len(shape) - 1 - dim))
    return level


def choose_distinct(key, rows, number_of, top, lift):
    order = jax.random.permutation(jax.random.fold_in(key, 1), number_of)
    pull = order
    for power in range(3):
        pull = pull * pull // number_of
    pull = pull * lift // number_of
    chance = jax.random.randint(jax.random.fold_in(key, 2), (rows, number_of), 0, 4096) + pull
    holders = jax.random.permutation(jax.random.fold_in(key, 3), rows)[jnp.arange(number_of) % rows]
    chance = jnp.where(jnp.arange(rows)[:, None] == holders[None, :], 1 << 14, chance)
    priority = chance * number_of + jnp.arange(number_of)
    return lax.top_k(priority.astype(jnp.int32), top)[1].astype(jnp.int32)


def centred(stream_key, extent, spread, bound, pieces=(), dtype=jnp.bfloat16):
    drawn = jax.random.normal(stream_key, extent, jnp.float32) * spread
    if len(pieces) > 0:
        drawn = level_of(stream_key, extent, pieces, -0.22, 0.18) * drawn
    return jnp.clip(drawn, min=-bound, max=bound).astype(dtype)


def setup_inputs(seed: int = 0, part: int = 0) -> dict:
    keys = jax.random.split(jax.random.key(seed), 7)
    own_keys = jax.random.split(jax.random.fold_in(keys[6], part), 7)
    return {
        "acts": centred(own_keys[0], (TOKENS, D), 1.0, 6.0, ((0, 4), (1, 4))),
        "out_grad": centred(own_keys[1], (TOKENS, 2 * DKV), 0.25, 1.5, ((0, 4), (1, 4))),
        "tenant_ids": choose_distinct(own_keys[2], BLOCKS, TENANTS, 1, 4096),
        "slot_map": jax.random.permutation(own_keys[3], TENANTS).astype(jnp.int32),
        "down_pool": centred(own_keys[4], (TENANTS, D, 2 * R), D ** -0.5, 0.0625, ((0, 4),)),
        "up_pool": centred(own_keys[5], (TENANTS, R, 2 * DKV), R ** -0.5, 0.75, ((0, 4),)),
    }


def reference(acts, out_grad, tenant_ids, slot_map, down_pool, up_pool):
    slot_rows = slot_map[tenant_ids[:, 0]].astype(jnp.int32)
    acts_blocks = acts.reshape(BLOCKS, BLOCK, D)
    grad_blocks = out_grad.reshape(BLOCKS, BLOCK, 2 * DKV)

    def block_step(totals, inputs):
        down_total, up_total = totals
        acts_block, grad_block, slot = inputs
        down = down_pool[slot]
        upper = up_pool[slot]
        shrunk = jnp.dot(acts_block, down, preferred_element_type=jnp.float32).astype(jnp.bfloat16)
        d_key = jnp.dot(grad_block[:, :DKV], upper[:, :DKV].T, preferred_element_type=jnp.float32)
        d_value = jnp.dot(grad_block[:, DKV:], upper[:, DKV:].T, preferred_element_type=jnp.float32)
        d_shrunk = jnp.concatenate([d_key, d_value], axis=1).astype(jnp.bfloat16)
        d_acts = jnp.dot(d_shrunk, down.T, preferred_element_type=jnp.float32).astype(jnp.bfloat16)
        part_down = jnp.dot(acts_block.T, d_shrunk, preferred_element_type=jnp.float32)
        part_key = jnp.dot(shrunk[:, :R].T, grad_block[:, :DKV], preferred_element_type=jnp.float32)
        part_value = jnp.dot(shrunk[:, R:].T, grad_block[:, DKV:], preferred_element_type=jnp.float32)
        part_up = jnp.concatenate([part_key, part_value], axis=1)
        down_total = down_total.at[slot].add(part_down)
        up_total = up_total.at[slot].add(part_up)
        return (down_total, up_total), d_acts

    start = (jnp.zeros((TENANTS, D, 2 * R), jnp.float32), jnp.zeros((TENANTS, R, 2 * DKV), jnp.float32))
    totals, d_blocks = lax.scan(block_step, start, (acts_blocks, grad_blocks, slot_rows))
    acts_grad = d_blocks.reshape(TOKENS, D)
    return acts_grad, totals[0].astype(jnp.bfloat16), totals[1].astype(jnp.bfloat16)
```

```python
import functools

import jax
import jax.numpy as jnp
from jax import lax
from jax.experimental import pallas as pl
from jax.experimental.pallas import tpu as pltpu
from jax.sharding import PartitionSpec as P

DKV = 1024
R = 64
BLOCK = 128
BF = jnp.bfloat16
F32 = jnp.float32
VMEM_BYTES = 40 * 1024 * 1024


def params():
    return pltpu.CompilerParams(vmem_limit_bytes=VMEM_BYTES)


def cost(flops, moved):
    return pl.CostEstimate(flops=flops, bytes_accessed=moved, transcendentals=0)


def back_kernel(pool_count, rel_ref, up_ref, grad_ref, out_ref):
    wide = lax.dot_general(
        up_ref[...], grad_ref[...], (((1,), (1,)), ((), ())), preferred_element_type=F32
    )
    rel = rel_ref[...]
    total = jnp.zeros(out_ref.shape, F32)
    for m in range(pool_count):
        total += jnp.where(rel == m, wide[m * R : (m + 1) * R], 0.0)
    out_ref[...] = total


def back_call(rel_rows, up_stack, out_grad, tile=512):
    rows, cols = out_grad.shape
    wide = up_stack.shape[0]
    return pl.pallas_call(
        functools.partial(back_kernel, wide // R),
        grid=(rows // tile,),
        out_shape=jax.ShapeDtypeStruct((R, rows), F32),
        in_specs=[
            pl.BlockSpec((1, tile), lambda i: (0, i)),
            pl.BlockSpec((wide, cols), lambda i: (0, 0)),
            pl.BlockSpec((tile, cols), lambda i: (i, 0)),
        ],
        out_specs=pl.BlockSpec((R, tile), lambda i: (0, i)),
        compiler_params=params(),
        cost_estimate=cost(2 * rows * cols * wide, rows * cols * 2),
    )(rel_rows, up_stack, out_grad)


def outer_kernel(pool_count, rel_ref, rank_ref, wide_ref, out_ref, lhs):
    @pl.when(pl.program_id(0) == 0)
    def _():
        rel = rel_ref[...]
        rank = rank_ref[...].astype(F32)
        for m in range(pool_count):
            lhs[m * R : (m + 1) * R, :] = jnp.where(rel == m, rank, 0.0).astype(BF)

    out_ref[...] = jnp.dot(lhs[...], wide_ref[...], preferred_element_type=F32).astype(BF)


def outer_call(rel_rows, rank_t, wide, pool_count, start, width, tile=256):
    rows = wide.shape[0]
    first = start // tile
    return pl.pallas_call(
        functools.partial(outer_kernel, pool_count),
        grid=(width // tile,),
        out_shape=jax.ShapeDtypeStruct((pool_count * R, width), BF),
        in_specs=[
            pl.BlockSpec((1, rows), lambda i: (0, 0)),
            pl.BlockSpec((R, rows), lambda i: (0, 0)),
            pl.BlockSpec((rows, tile), lambda i: (0, first + i)),
        ],
        out_specs=pl.BlockSpec((pool_count * R, tile), lambda i: (0, i)),
        scratch_shapes=[pltpu.VMEM((pool_count * R, rows), BF)],
        compiler_params=params(),
        cost_estimate=cost(2 * rows * pool_count * R * width, rows * width * 2),
    )(rel_rows, rank_t, wide)


def load_pool(pools, held, sems):
    copies = [pltpu.make_async_copy(p, held.at[m], sems.at[m]) for m, p in enumerate(pools)]
    for c in copies:
        c.start()
    for c in copies:
        c.wait()


def shrink_kernel(pool_count, per, rel_ref, *refs):
    pools = refs[:pool_count]
    acts_ref, out_ref, held, sems = refs[pool_count:]
    i = pl.program_id(0)

    @pl.when(i == 0)
    def _():
        load_pool(pools, held, sems)

    for b in range(per):
        part = jnp.dot(
            acts_ref[b * BLOCK : (b + 1) * BLOCK, :],
            held[rel_ref[i * per + b]],
            preferred_element_type=F32,
        )
        out_ref[:, b * BLOCK : (b + 1) * BLOCK] = part.T


def shrink_call(rel, pools, acts, per=4):
    rows, width = acts.shape
    count = len(pools)
    return pl.pallas_call(
        functools.partial(shrink_kernel, count, per),
        grid_spec=pltpu.PrefetchScalarGridSpec(
            num_scalar_prefetch=1,
            grid=(rows // (BLOCK * per),),
            in_specs=[pl.BlockSpec(memory_space=pl.ANY)] * count
            + [pl.BlockSpec((per * BLOCK, width), lambda i, rel: (i, 0))],
            out_specs=pl.BlockSpec((2 * R, per * BLOCK), lambda i, rel: (0, i)),
            scratch_shapes=[
                pltpu.VMEM((count, width, 2 * R), BF),
                pltpu.SemaphoreType.DMA((count,)),
            ],
        ),
        out_shape=jax.ShapeDtypeStruct((2 * R, rows), F32),
        compiler_params=params(),
        cost_estimate=cost(4 * rows * width * 2 * R, rows * width * 2),
    )(rel, *pools, acts)


def expand_kernel(pool_count, per, rel_ref, *refs):
    pools = refs[:pool_count]
    rank_ref, out_ref, held, sems = refs[pool_count:]
    i = pl.program_id(0)

    @pl.when(i == 0)
    def _():
        load_pool(pools, held, sems)

    for b in range(per):
        rank = rank_ref[:, b * BLOCK : (b + 1) * BLOCK].astype(F32).T.astype(BF)
        out_ref[b * BLOCK : (b + 1) * BLOCK, :] = lax.dot_general(
            rank, held[rel_ref[i * per + b]], (((1,), (1,)), ((), ())), preferred_element_type=F32
        ).astype(BF)


def expand_call(rel, pools, rank_t, width, per=4):
    rows = rank_t.shape[1]
    count = len(pools)
    return pl.pallas_call(
        functools.partial(expand_kernel, count, per),
        grid_spec=pltpu.PrefetchScalarGridSpec(
            num_scalar_prefetch=1,
            grid=(rows // (BLOCK * per),),
            in_specs=[pl.BlockSpec(memory_space=pl.ANY)] * count
            + [pl.BlockSpec((2 * R, per * BLOCK), lambda i, rel: (0, i))],
            out_specs=pl.BlockSpec((per * BLOCK, width), lambda i, rel: (i, 0)),
            scratch_shapes=[
                pltpu.VMEM((count, width, 2 * R), BF),
                pltpu.SemaphoreType.DMA((count,)),
            ],
        ),
        out_shape=jax.ShapeDtypeStruct((rows, width), BF),
        compiler_params=params(),
        cost_estimate=cost(4 * rows * width * 2 * R, rows * width * 2),
    )(rel, *pools, rank_t)


def place_kernel(count, start, has_input, pos_ref, *refs):
    first, second = refs[:count], refs[count : 2 * count]
    rest = refs[2 * count + (1 if has_input else 0) :]
    out_ref, turned, sems = rest
    width = first[0].shape[1]
    copies = []
    for m in range(count):
        sender = pos_ref[0] ^ m
        swap = sender >= count // 2
        a, b = first[m][...].astype(F32), second[m][...].astype(F32)
        turned[m, :, :] = jnp.concatenate(
            [jnp.where(swap, b, a), jnp.where(swap, a, b)], axis=0
        ).T.astype(BF)
        row = pl.multiple_of(sender * (out_ref.shape[0] // count) + start, 128)
        copy = pltpu.make_async_copy(turned.at[m], out_ref.at[pl.ds(row, width), :], sems.at[m])
        copy.start()
        copies.append(copy)
    for copy in copies:
        copy.wait()


def place_call(position, first, second, start, total_rows, held):
    count = len(first)
    width = first[0].shape[1]
    whole = pl.BlockSpec(memory_space=pltpu.VMEM)
    extra = [] if held is None else [held]
    return pl.pallas_call(
        functools.partial(place_kernel, count, start, held is not None),
        out_shape=jax.ShapeDtypeStruct((total_rows, 2 * R), BF),
        in_specs=[pl.BlockSpec(memory_space=pltpu.SMEM)]
        + [whole] * (2 * count)
        + [pl.BlockSpec(memory_space=pl.ANY)] * len(extra),
        out_specs=pl.BlockSpec(memory_space=pl.ANY),
        scratch_shapes=[
            pltpu.VMEM((count, width, 2 * R), BF),
            pltpu.SemaphoreType.DMA((count,)),
        ],
        input_output_aliases={} if held is None else {1 + 2 * count: 0},
        compiler_params=params(),
        cost_estimate=cost(0, 4 * count * width * 2 * R * 2),
    )(position.reshape(1), *first, *second, *extra)


def local(acts, out_grad, tenant_ids, slot_map, down_pool, up_pool):
    count = lax.axis_size("adapter")
    j = lax.axis_index("adapter")
    z = lax.axis_index("dp")
    rows, width = acts.shape
    cols = out_grad.shape[1]
    total_rows = down_pool.shape[1]
    upper = j >= count // 2

    def swap(x, m):
        return lax.ppermute(x, "adapter", [(i, i ^ m) for i in range(count)])

    rel = jnp.bitwise_xor(slot_map[tenant_ids[:, 0]], j).astype(jnp.int32)
    rel_rows = jnp.repeat(rel, BLOCK)[None, :]

    def up_piece(m):
        return lax.dynamic_slice(up_pool[0], (0, (j ^ m) * cols), (R, cols))

    def down_piece(m):
        return lax.dynamic_slice(down_pool[0], ((j ^ m) * width, 0), (width, 2 * R))

    ups = [up_piece(0)] + [swap(up_piece(m), m) for m in range(1, count)]
    pools = [down_piece(0)] + [swap(down_piece(m), m) for m in range(1, count)]
    up_stack = jnp.concatenate(ups, axis=0)

    back_part = back_call(rel_rows, up_stack, out_grad)
    d_own = (back_part + swap(back_part, 1)).astype(BF)
    d_other = swap(d_own, 2)

    chunk = 512
    pieces = width // chunk
    own = [outer_call(rel_rows, d_own, acts, count, c * chunk, chunk) for c in range(pieces)]
    other = [outer_call(rel_rows, d_other, acts, count, c * chunk, chunk) for c in range(pieces)]

    shrunk_part = shrink_call(rel, pools, acts)
    shrunk_sum = shrunk_part + swap(shrunk_part, 1)
    key, value = shrunk_sum[:R], shrunk_sum[R:]
    came = swap(jnp.where(upper, key, value).astype(BF), 2)
    shrunk_own = (jnp.where(upper, value, key) + came.astype(F32)).astype(BF)
    up_part = outer_call(rel_rows, shrunk_own, out_grad, count, 0, cols)

    d_full = jnp.where(
        upper,
        jnp.concatenate([d_other, d_own], axis=0),
        jnp.concatenate([d_own, d_other], axis=0),
    )
    acts_grad = expand_call(rel, pools, d_full, width)

    names = [("own", c) for c in range(pieces)] + [("other", c) for c in range(pieces - 1)]
    names += [("up", 0), ("other", pieces - 1)]
    stream = {("own", c): own[c] for c in range(pieces)}
    stream.update({("other", c): other[c] for c in range(pieces)})
    stream[("up", 0)] = up_part
    parts = [stream[n] for n in names]
    n_parts = len(parts)
    edge = (z == 0) | (z == 3)
    lag = 4
    inner, total, final = {}, {}, {}
    for t in range(n_parts + lag):
        back = t - lag
        if back >= 0:
            came = lax.ppermute(inner[back], "dp", [(1, 2), (2, 1)])
            total[back] = (inner[back].astype(F32) + came.astype(F32)).astype(BF)
        if t < n_parts and back >= 0:
            payload = jnp.where(edge, parts[t], total[back])
        elif t < n_parts:
            payload = parts[t]
        else:
            payload = total[back]
        got = lax.ppermute(payload, "dp", [(0, 1), (1, 0), (2, 3), (3, 2)])
        if t < n_parts:
            inner[t] = (parts[t].astype(F32) + got.astype(F32)).astype(BF)
        if back >= 0:
            final[names[back]] = jnp.where(edge, got, total[back])

    def to_owner(x):
        return [x[:R]] + [swap(x[m * R : (m + 1) * R], m) for m in range(1, count)]

    down_grad = None
    own_pairs = [
        to_owner(jnp.concatenate([final[("own", c)], final[("own", c + 1)]], axis=1))
        for c in range(0, pieces, 2)
    ]
    for c in range(pieces):
        first = [p[:, (c % 2) * chunk : (c % 2 + 1) * chunk] for p in own_pairs[c // 2]]
        second = to_owner(final[("other", c)])
        down_grad = place_call(j, first, second, c * chunk, total_rows, down_grad)

    up_pieces = to_owner(final[("up", 0)])
    up_grad = jnp.zeros((R, cols * count), BF)
    for m in range(count):
        up_grad = lax.dynamic_update_slice(up_grad, up_pieces[m], (0, (j ^ m) * cols))
    return acts_grad, down_grad[None], up_grad[None]


def local_any(acts, out_grad, tenant_ids, slot_map, down_pool, up_pool):
    position = lax.axis_index("adapter")
    row_count, local_width = acts.shape
    col_count = out_grad.shape[1]
    block_count = row_count // BLOCK
    tenant_slot = slot_map[tenant_ids[:, 0]]
    down_slices = lax.all_to_all(down_pool, "adapter", split_axis=1, concat_axis=0, tiled=True)
    up_slices = lax.all_to_all(up_pool, "adapter", split_axis=2, concat_axis=0, tiled=True)
    tenant_count = down_slices.shape[0]
    acts_blocks = acts.reshape(block_count, BLOCK, local_width)
    grad_blocks = out_grad.reshape(block_count, BLOCK, col_count)
    down_blocks = down_slices[tenant_slot]
    up_blocks = up_slices[tenant_slot]
    shrunk_part = jnp.einsum(
        "bnd,bdr->bnr", acts_blocks, down_blocks, preferred_element_type=jnp.float32
    )
    back_part = jnp.einsum(
        "bnc,brc->bnr", grad_blocks, up_blocks, preferred_element_type=jnp.float32
    )
    is_key = position * col_count < DKV
    zero_part = jnp.zeros_like(back_part)
    d_part = jnp.where(
        is_key,
        jnp.concatenate([back_part, zero_part], axis=-1),
        jnp.concatenate([zero_part, back_part], axis=-1),
    )
    shrunk_sum, d_sum = lax.psum((shrunk_part, d_part), "adapter")
    shrunk = shrunk_sum.astype(jnp.bfloat16)
    d_shrunk = d_sum.astype(jnp.bfloat16)
    acts_grad = jnp.einsum(
        "bnr,bdr->bnd", d_shrunk, down_blocks, preferred_element_type=jnp.float32
    )
    acts_grad = acts_grad.astype(jnp.bfloat16).reshape(row_count, local_width)
    part_down = jnp.einsum(
        "bnd,bnr->bdr", acts_blocks, d_shrunk, preferred_element_type=jnp.float32
    )
    own_shrunk = jnp.where(is_key, shrunk[..., :R], shrunk[..., R:])
    part_up = jnp.einsum(
        "bnr,bnc->brc", own_shrunk, grad_blocks, preferred_element_type=jnp.float32
    )
    member = (tenant_slot[None, :] == jnp.arange(tenant_count, dtype=jnp.int32)[:, None]).astype(
        jnp.float32
    )
    grad_down = jnp.einsum("tb,bdr->tdr", member, part_down, precision=lax.Precision.HIGHEST)
    grad_up = jnp.einsum("tb,brc->trc", member, part_up, precision=lax.Precision.HIGHEST)
    owned_down = lax.all_to_all(grad_down, "adapter", split_axis=0, concat_axis=1, tiled=True)
    owned_up = lax.all_to_all(grad_up, "adapter", split_axis=0, concat_axis=2, tiled=True)
    total_down, total_up = lax.psum((owned_down, owned_up), "dp")
    down_grad = total_down.astype(jnp.bfloat16)
    up_grad = total_up.astype(jnp.bfloat16)
    return (acts_grad, down_grad, up_grad)


def solution(mesh):
    small = mesh.shape["adapter"] == 4 and mesh.shape["dp"] == 4
    return jax.shard_map(
        local if small else local_any,
        mesh=mesh,
        in_specs=(
            P(("groups", "dp"), "adapter"),
            P(("groups", "dp"), "adapter"),
            P(("groups", "dp"), None),
            P("groups"),
            P(("groups", "adapter"), None, None),
            P(("groups", "adapter"), None, None),
        ),
        out_specs=(
            P(("groups", "dp"), "adapter"),
            P(("groups", "adapter"), None, None),
            P(("groups", "adapter"), None, None),
        ),
        check_vma=False,
    )
```

```python
import jax
import jax.numpy as jnp
from jax import lax
from jax.experimental import pallas as pl
from jax.experimental.pallas import tpu as pltpu
from jax.sharding import PartitionSpec as P

DKV = 1024
R = 64
BLOCK = 128
BF = jnp.bfloat16
F32 = jnp.float32
WHOLE = pl.BlockSpec(memory_space=pltpu.VMEM)
SCALARS = pl.BlockSpec(memory_space=pltpu.SMEM)
FAR = pl.BlockSpec(memory_space=pltpu.HBM)
EDGE, UPPER, ODD, PLACE = range(4)


def launch(body, args, specs, outs, out_specs, scratch, mib, flops, moved, marks, grid=()):
    n_in, n_args, n_outs = len(args) + len(marks), len(args), len(outs)

    def kernel(*refs):
        refs[n_in + n_outs][...] = jnp.zeros((8, 128), F32)
        body(*refs[:n_args], *refs[n_in : n_in + n_outs], *refs[n_in + n_outs + 1 :])

    return pl.pallas_call(
        kernel,
        grid=grid,
        out_shape=[*outs, jax.ShapeDtypeStruct((8, 128), F32)],
        in_specs=[*specs, *[pl.BlockSpec(memory_space=pl.ANY)] * len(marks)],
        out_specs=[*out_specs, WHOLE],
        scratch_shapes=scratch,
        compiler_params=pltpu.CompilerParams(vmem_limit_bytes=mib * 1024 * 1024),
        cost_estimate=pl.CostEstimate(flops=flops, bytes_accessed=moved, transcendentals=0),
    )(*args, *marks)


def back_call(flags, slot_rows, up_stack, out_grad, marks, pieces=4):
    rows, cols = out_grad.shape
    wide = up_stack.shape[0]
    depth = rows // pieces

    def body(flag_ref, slot_ref, up_ref, grad_ref, out_ref, held, sems):
        copies = []
        for p in range(pieces):
            here = pl.ds(p * depth, depth)
            copies.append(pltpu.make_async_copy(grad_ref.at[here, :], held.at[p], sems.at[p]))
            copies[-1].start()
        for p in range(pieces):
            copies[p].wait()
            here = slice(p * depth, (p + 1) * depth)
            every = lax.dot_general(
                up_ref[...], held[p], (((1,), (1,)), ((), ())), preferred_element_type=F32
            )
            rel = jnp.bitwise_xor(slot_ref[:, here], flag_ref[PLACE])
            total = jnp.zeros((R, depth), F32)
            for m in range(wide // R):
                total += jnp.where(rel == m, every[m * R : (m + 1) * R], 0.0)
            out_ref[:, here] = total

    return launch(
        body,
        (flags, slot_rows, up_stack, out_grad),
        (SCALARS, WHOLE, WHOLE, FAR),
        (jax.ShapeDtypeStruct((R, rows), F32),),
        (WHOLE,),
        [pltpu.VMEM((pieces, depth, cols), BF), pltpu.SemaphoreType.DMA((pieces,))],
        8,
        2 * rows * cols * wide,
        rows * cols * 2,
        marks,
    )


def outer_call(kind, flags, slot_rows, ranks, wide, count, starts, width, marks, pieces=4):
    rows = wide.shape[0]
    depth = rows // pieces
    n = len(starts)
    half = rows // 2
    n_extra = {"sum": 2, "halves": 1, "whole": 0, "late": 0}[kind]

    def body(flag_ref, slot_ref, *refs):
        rank_refs = refs[: len(ranks)]
        wide_ref = refs[len(ranks)]
        outs = refs[len(ranks) + 1 : len(ranks) + 1 + n]
        extra = refs[len(ranks) + 1 + n : len(ranks) + 1 + n + n_extra]
        lhs, held, sems = refs[-3:]

        def copy(i, p):
            return pltpu.make_async_copy(
                wide_ref.at[pl.ds(p * depth, depth), pl.ds(starts[i], width)],
                held.at[i, p],
                sems.at[i, p],
            )

        for i in range(n):
            for p in range(pieces):
                copy(i, p).start()
        odd = flag_ref[ODD] == 1
        if kind in ("sum", "late"):
            rank = rank_refs[0][...] + rank_refs[1][...].astype(F32)
        elif kind == "halves":
            mine, theirs = rank_refs[0][...].astype(F32), rank_refs[1][...].astype(F32)
            first = jnp.where(odd, theirs, mine)
            second = jnp.where(odd, mine, theirs)
            rank = jnp.concatenate([first, second], axis=1)
        else:
            rank = rank_refs[0][...].astype(F32)
        if kind in ("sum", "halves"):
            extra[0][...] = rank.astype(BF)
        if kind == "sum":
            extra[1][...] = jnp.where(odd, rank[:, half:], rank[:, :half]).astype(BF)
        slot = slot_ref[...]
        for m in range(count):
            lhs[m * R : (m + 1) * R, :] = jnp.where(slot == m, rank, 0.0).astype(BF)
        for i in range(n):
            total = jnp.zeros(outs[i].shape, F32)
            for p in range(pieces):
                copy(i, p).wait()
                total += jnp.dot(
                    lhs[:, p * depth : (p + 1) * depth], held[i, p], preferred_element_type=F32
                )
            outs[i][...] = total.astype(BF)

    outs = [jax.ShapeDtypeStruct((count * R, width), BF)] * n
    outs += [jax.ShapeDtypeStruct((R, rows), BF), jax.ShapeDtypeStruct((R, half), BF)][:n_extra]
    return launch(
        body,
        (flags, slot_rows, *ranks, wide),
        (SCALARS, WHOLE, *[WHOLE] * len(ranks), FAR),
        outs,
        [WHOLE] * len(outs),
        [
            pltpu.VMEM((count * R, rows), BF),
            pltpu.VMEM((n, pieces, depth, width), BF),
            pltpu.SemaphoreType.DMA((n, pieces)),
        ],
        7 + 2 * n,
        2 * rows * count * R * width * n,
        rows * width * 2 * n,
        marks,
    )


def shrink_call(slot, pool, acts, marks, per=4):
    rows, width = acts.shape

    def body(slot_ref, pool_ref, acts_ref, out_ref):
        i = pl.program_id(0)
        for b in range(per):
            here = slice(b * BLOCK, (b + 1) * BLOCK)
            part = jnp.dot(
                acts_ref[here, :], pool_ref[slot_ref[i * per + b]], preferred_element_type=F32
            )
            out_ref[:, here] = part.T

    return launch(
        body,
        (slot, pool, acts),
        (SCALARS, WHOLE, pl.BlockSpec((per * BLOCK, width), lambda i: (i, 0))),
        (jax.ShapeDtypeStruct((2 * R, rows), F32),),
        (pl.BlockSpec((2 * R, per * BLOCK), lambda i: (0, i)),),
        [],
        12,
        4 * rows * width * 2 * R,
        rows * width * 2,
        marks,
        (rows // (BLOCK * per),),
    )


def mix_call(flags, part, peer, marks):
    rows = part.shape[1]

    def body(flag_ref, part_ref, peer_ref, keep_ref, send_ref):
        upper = flag_ref[UPPER] == 1
        key = part_ref[:R] + peer_ref[:R]
        value = part_ref[R:] + peer_ref[R:]
        keep_ref[...] = jnp.where(upper, value, key)
        send_ref[...] = jnp.where(upper, key, value).astype(BF)

    return launch(
        body,
        (flags, part, peer),
        (SCALARS, WHOLE, WHOLE),
        (jax.ShapeDtypeStruct((R, rows), F32), jax.ShapeDtypeStruct((R, rows), BF)),
        (WHOLE, WHOLE),
        [],
        6,
        1,
        rows * R * 16,
        marks,
    )


def expand_call(flags, slot, pool, own, other, width, marks, per=4):
    rows = own.shape[1]

    def body(flag_ref, slot_ref, pool_ref, own_ref, other_ref, out_ref):
        i = pl.program_id(0)
        upper = flag_ref[UPPER] == 1
        for b in range(per):
            here = slice(b * BLOCK, (b + 1) * BLOCK)
            mine, theirs = own_ref[:, here].astype(F32), other_ref[:, here].astype(F32)
            rank = jnp.concatenate(
                [jnp.where(upper, theirs, mine), jnp.where(upper, mine, theirs)], axis=0
            )
            out_ref[here, :] = lax.dot_general(
                rank.T.astype(BF),
                pool_ref[slot_ref[i * per + b]],
                (((1,), (1,)), ((), ())),
                preferred_element_type=F32,
            ).astype(BF)

    return launch(
        body,
        (flags, slot, pool, own, other),
        (
            SCALARS,
            SCALARS,
            WHOLE,
            pl.BlockSpec((R, per * BLOCK), lambda i: (0, i)),
            pl.BlockSpec((R, per * BLOCK), lambda i: (0, i)),
        ),
        (pltpu.HBM((rows, width), BF),),
        (pl.BlockSpec((per * BLOCK, width), lambda i: (i, 0)),),
        [],
        12,
        4 * rows * width * 2 * R,
        rows * width * 2,
        marks,
        (rows // (BLOCK * per),),
    )


def place_call(first, second, start, total_rows, held):
    count = first.shape[0] // R
    width = first.shape[1]
    extra = [] if held is None else [held]

    def kernel(first_ref, second_ref, *refs):
        out_ref, turned, sems = refs[-3:]
        copies = []
        for m in range(count):
            rows = slice(m * R, (m + 1) * R)
            a, b = first_ref[rows].astype(F32), second_ref[rows].astype(F32)
            pair = [a, b] if m < count // 2 else [b, a]
            turned[m, :, :] = jnp.concatenate(pair, axis=0).T.astype(BF)
            row = m * (total_rows // count) + start
            copies.append(
                pltpu.make_async_copy(
                    turned.at[m], out_ref.at[pl.ds(row, width), :], sems.at[m]
                )
            )
            copies[-1].start()
        for copy in copies:
            copy.wait()

    return pl.pallas_call(
        kernel,
        out_shape=jax.ShapeDtypeStruct((total_rows, 2 * R), BF),
        in_specs=[WHOLE, WHOLE] + [pl.BlockSpec(memory_space=pl.ANY)] * len(extra),
        out_specs=pl.BlockSpec(memory_space=pl.ANY),
        scratch_shapes=[
            pltpu.VMEM((count, width, 2 * R), BF),
            pltpu.SemaphoreType.DMA((count,)),
        ],
        input_output_aliases={} if held is None else {2: 0},
        compiler_params=pltpu.CompilerParams(vmem_limit_bytes=10 * 1024 * 1024),
        cost_estimate=pl.CostEstimate(
            flops=1, bytes_accessed=4 * count * width * 2 * R * 2, transcendentals=0
        ),
    )(first, second, *extra)


def step_call(flags, arrays, outs, shape, marks):
    names = list(arrays)

    def body(flag_ref, *refs):
        got = dict(zip(names, refs[: len(names)]))
        put = dict(zip(outs, refs[len(names) :]))
        edge = flag_ref[EDGE] == 1

        def add(a, b):
            return (got[a][...].astype(F32) + got[b][...].astype(F32)).astype(BF)

        if "inner" in put:
            put["inner"][...] = add("old_part", "from_line")
        if "line" in put:
            if "old_inner" in got and "part" in got:

                @pl.when(edge)
                def _():
                    put["line"][...] = got["part"][...]

                @pl.when(jnp.logical_not(edge))
                def _():
                    put["line"][...] = add("old_inner", "from_inner")

            elif "old_inner" in got:
                put["line"][...] = add("old_inner", "from_inner")
            else:
                put["line"][...] = got["part"][...]
        if "final" in put:

            @pl.when(edge)
            def _():
                put["final"][...] = got["from_line"][...]

            @pl.when(jnp.logical_not(edge))
            def _():
                put["final"][...] = got["old_line"][...]

    made = launch(
        body,
        (flags, *arrays.values()),
        (SCALARS, *[WHOLE] * len(names)),
        [jax.ShapeDtypeStruct(shape, BF)] * len(outs),
        [WHOLE] * len(outs),
        [],
        6,
        1,
        12 * shape[0] * shape[1],
        marks,
    )
    return dict(zip([*outs, "mark"], made))


def local(acts, out_grad, tenant_ids, slot_map, down_pool, up_pool):
    acts = pltpu.with_memory_space_constraint(acts, pltpu.HBM)
    out_grad = pltpu.with_memory_space_constraint(out_grad, pltpu.HBM)
    count = lax.axis_size("adapter")
    j = lax.axis_index("adapter")
    z = lax.axis_index("dp")
    rows, width = acts.shape
    cols = out_grad.shape[1]
    total_rows = down_pool.shape[1]
    edge = (z == 0) | (z == 3)
    flags = jnp.stack([edge.astype(jnp.int32), j // (count // 2), j % 2, j]).astype(jnp.int32)

    def swap(x, m):
        return lax.ppermute(x, "adapter", [(i, i ^ m) for i in range(count)])

    def to_owner(x):
        return lax.all_to_all(x, "adapter", split_axis=0, concat_axis=0, tiled=True)

    slot = slot_map[tenant_ids[:, 0]].astype(jnp.int32)
    slot_rows = jnp.repeat(slot, BLOCK)[None, :]

    def up_piece(m):
        return lax.dynamic_slice(up_pool[0], (0, (j ^ m) * cols), (R, cols))

    ups = [up_piece(0)] + [swap(up_piece(m), m) for m in range(1, count)]
    back_part, mark = back_call(flags, slot_rows, jnp.concatenate(ups, axis=0), out_grad, [])
    back_peer = swap(back_part, 1)

    chunk = 512
    names = ["own0", "own1", "own2", "own3", "other0", "other1", "other2", "other3", "up"]
    n = len(names)
    parts, line, inner, from_line, from_inner, final = {}, {}, {}, {}, {}, {}

    def joined(*which):
        return jnp.concatenate([final[w] for w in which], axis=1)

    for t in range(n + 6):
        if t == 0:
            parts["own0"], d_own, d_half, mark = outer_call(
                "sum", flags, slot_rows, [back_part, back_peer], acts, count, [0], chunk, []
            )
            came_half = swap(d_half, 2)
            came_other = swap(came_half, 1)
            pool_in, _ = lax.optimization_barrier((down_pool[0], came_half))
            pool = to_owner(pool_in).reshape(count, width, 2 * R)
            pool = pltpu.with_memory_space_constraint(pool, pltpu.HBM)
        if t == 1:
            starts = [chunk, 2 * chunk, 3 * chunk]
            parts["own1"], parts["own2"], parts["own3"], mark = outer_call(
                "whole", flags, slot_rows, [d_own], acts, count, starts, chunk, [mark]
            )
        if t == 4:
            starts = [0, chunk, 2 * chunk, 3 * chunk]
            made = outer_call(
                "halves", flags, slot_rows, [came_half, came_other], acts, count, starts, chunk,
                [mark],
            )
            parts.update({"other%d" % c: made[c] for c in range(4)})
            d_other, mark = made[4:]
        if t == 7:
            shrunk_part, mark = shrink_call(slot, pool, acts, [mark])
            shrunk_peer = swap(shrunk_part, 1)
        if t == 8:
            keep, send, mark = mix_call(flags, shrunk_part, shrunk_peer, [mark])
            parts["up"], mark = outer_call(
                "late", flags, slot_rows, [keep, swap(send, 2)], out_grad, count, [0], cols, [mark]
            )
        if t == 13:
            acts_grad, mark = expand_call(
                flags, slot, pool, d_own, d_other, width, [mark]
            )
        if t < 2:
            line[t] = parts[names[t]]
        else:
            arrays, outs = {}, []
            if t < n:
                arrays["part"] = parts[names[t]]
            if t - 2 < n or t >= 6:
                arrays["from_line"] = from_line[t - 2]
            if t - 2 < n:
                arrays["old_part"] = parts[names[t - 2]]
                outs.append("inner")
            if 0 <= t - 4 < n:
                arrays["old_inner"] = inner[t - 2]
                arrays["from_inner"] = from_inner[t - 2]
            if t < n or 0 <= t - 4 < n:
                outs.append("line")
            if 0 <= t - 6 < n:
                arrays["old_line"] = line[t - 2]
                outs.append("final")
            marks = [mark, came_half] if t == 2 else [mark]
            made = step_call(flags, arrays, outs, (count * R, chunk), marks)
            mark = made["mark"]
            if "inner" in made:
                inner[t] = made["inner"]
            if "line" in made:
                line[t] = made["line"]
            if "final" in made:
                final[names[t - 6]] = made["final"]
        if t in line:
            from_line[t] = lax.ppermute(line[t], "dp", [(0, 1), (1, 0), (2, 3), (3, 2)])
        if t in inner:
            from_inner[t] = lax.ppermute(inner[t], "dp", [(1, 2), (2, 1)])

    split = 3 * chunk
    own = to_owner(joined("own0", "own1", "own2", "own3"))
    three = to_owner(joined("other0", "other1", "other2"))
    last = to_owner(joined("other3", "up"))
    down_grad = place_call(own[:, :split], three, 0, total_rows, None)
    down_grad = place_call(own[:, split:], last[:, :chunk], split, total_rows, down_grad)
    up_got = last[:, chunk:].reshape(count, R, cols)
    up_grad = jnp.concatenate([up_got[m] for m in range(count)], axis=1)
    return acts_grad, down_grad[None], up_grad[None]


def local_any(acts, out_grad, tenant_ids, slot_map, down_pool, up_pool):
    position = lax.axis_index("adapter")
    row_count, local_width = acts.shape
    col_count = out_grad.shape[1]
    block_count = row_count // BLOCK
    tenant_slot = slot_map[tenant_ids[:, 0]]
    down_slices = lax.all_to_all(down_pool, "adapter", split_axis=1, concat_axis=0, tiled=True)
    up_slices = lax.all_to_all(up_pool, "adapter", split_axis=2, concat_axis=0, tiled=True)
    tenant_count = down_slices.shape[0]
    acts_blocks = acts.reshape(block_count, BLOCK, local_width)
    grad_blocks = out_grad.reshape(block_count, BLOCK, col_count)
    down_blocks = down_slices[tenant_slot]
    up_blocks = up_slices[tenant_slot]
    shrunk_part = jnp.einsum(
        "bnd,bdr->bnr", acts_blocks, down_blocks, preferred_element_type=jnp.float32
    )
    back_part = jnp.einsum(
        "bnc,brc->bnr", grad_blocks, up_blocks, preferred_element_type=jnp.float32
    )
    is_key = position * col_count < DKV
    zero_part = jnp.zeros_like(back_part)
    d_part = jnp.where(
        is_key,
        jnp.concatenate([back_part, zero_part], axis=-1),
        jnp.concatenate([zero_part, back_part], axis=-1),
    )
    shrunk_sum, d_sum = lax.psum((shrunk_part, d_part), "adapter")
    shrunk = shrunk_sum.astype(jnp.bfloat16)
    d_shrunk = d_sum.astype(jnp.bfloat16)
    acts_grad = jnp.einsum(
        "bnr,bdr->bnd", d_shrunk, down_blocks, preferred_element_type=jnp.float32
    )
    acts_grad = acts_grad.astype(jnp.bfloat16).reshape(row_count, local_width)
    part_down = jnp.einsum(
        "bnd,bnr->bdr", acts_blocks, d_shrunk, preferred_element_type=jnp.float32
    )
    own_shrunk = jnp.where(is_key, shrunk[..., :R], shrunk[..., R:])
    part_up = jnp.einsum(
        "bnr,bnc->brc", own_shrunk, grad_blocks, preferred_element_type=jnp.float32
    )
    member = (tenant_slot[None, :] == jnp.arange(tenant_count, dtype=jnp.int32)[:, None]).astype(
        jnp.float32
    )
    grad_down = jnp.einsum("tb,bdr->tdr", member, part_down, precision=lax.Precision.HIGHEST)
    grad_up = jnp.einsum("tb,brc->trc", member, part_up, precision=lax.Precision.HIGHEST)
    owned_down = lax.all_to_all(grad_down, "adapter", split_axis=0, concat_axis=1, tiled=True)
    owned_up = lax.all_to_all(grad_up, "adapter", split_axis=0, concat_axis=2, tiled=True)
    total_down, total_up = lax.psum((owned_down, owned_up), "dp")
    down_grad = total_down.astype(jnp.bfloat16)
    up_grad = total_up.astype(jnp.bfloat16)
    return (acts_grad, down_grad, up_grad)


def solution(mesh):
    line_of_four = mesh.shape["adapter"] == 4 and mesh.shape["dp"] == 4
    return jax.shard_map(
        local if line_of_four else local_any,
        mesh=mesh,
        in_specs=(
            P(("groups", "dp"), "adapter"),
            P(("groups", "dp"), "adapter"),
            P(("groups", "dp"), None),
            P("groups"),
            P(("groups", "adapter"), None, None),
            P(("groups", "adapter"), None, None),
        ),
        out_specs=(
            P(("groups", "dp"), "adapter"),
            P(("groups", "adapter"), None, None),
            P(("groups", "adapter"), None, None),
        ),
        check_vma=False,
    )
```

```python
import jax
import jax.numpy as jnp
from jax import lax
from jax.experimental import pallas as pl
from jax.experimental.pallas import tpu as pltpu
from jax.sharding import PartitionSpec as P

DKV = 1024
R = 64
BLOCK = 128
BF = jnp.bfloat16
F32 = jnp.float32
WHOLE = pl.BlockSpec(memory_space=pltpu.VMEM)
SCALARS = pl.BlockSpec(memory_space=pltpu.SMEM)
FAR = pl.BlockSpec(memory_space=pltpu.HBM)
EDGE, UPPER, ODD, PLACE, DP_PLACE = range(5)
(
    PART, FROM_LINE, OLD_PART, INNER, OLD_INNER, FROM_INNER, LINE, OLD_LINE, FINAL, FINALS,
    OLD_FINAL, WIDE, KEEP, SEND, SHRUNK_MINE, SHRUNK_THEIRS, KEPT, CAME, SLOT_ROWS,
    HALF_MINE, HALF_THEIRS, D_OTHER, RANK, MARK,
) = range(24)


def launch(body, args, specs, outs, out_specs, scratch, mib, flops, moved, marks, grid=()):
    n_in, n_args, n_outs = len(args) + len(marks), len(args), len(outs)

    def kernel(*refs):
        refs[n_in + n_outs][...] = jnp.zeros((8, 128), F32)
        body(*refs[:n_args], *refs[n_in : n_in + n_outs], *refs[n_in + n_outs + 1 :])

    return pl.pallas_call(
        kernel,
        grid=grid,
        out_shape=[*outs, jax.ShapeDtypeStruct((8, 128), F32)],
        in_specs=[*specs, *[pl.BlockSpec(memory_space=pl.ANY)] * len(marks)],
        out_specs=[*out_specs, WHOLE],
        scratch_shapes=scratch,
        compiler_params=pltpu.CompilerParams(vmem_limit_bytes=mib * 1024 * 1024),
        cost_estimate=pl.CostEstimate(flops=flops, bytes_accessed=moved, transcendentals=0),
    )(*args, *marks)


def back_call(flags, slot_rows, up_stack, out_grad, marks, pieces=4):
    rows, cols = out_grad.shape
    wide = up_stack.shape[0]
    depth = rows // pieces

    def body(flag_ref, slot_ref, up_ref, grad_ref, out_ref, held, sems):
        copies = []
        for p in range(pieces):
            here = pl.ds(p * depth, depth)
            copies.append(pltpu.make_async_copy(grad_ref.at[here, :], held.at[p], sems.at[p]))
            copies[-1].start()
        for p in range(pieces):
            copies[p].wait()
            here = slice(p * depth, (p + 1) * depth)
            every = lax.dot_general(
                up_ref[...], held[p], (((1,), (1,)), ((), ())), preferred_element_type=F32
            )
            rel = jnp.bitwise_xor(slot_ref[:, here], flag_ref[PLACE])
            total = jnp.zeros((R, depth), F32)
            for m in range(wide // R):
                total += jnp.where(rel == m, every[m * R : (m + 1) * R], 0.0)
            out_ref[:, here] = total

    return launch(
        body,
        (flags, slot_rows, up_stack, out_grad),
        (SCALARS, WHOLE, WHOLE, FAR),
        (jax.ShapeDtypeStruct((R, rows), F32),),
        (WHOLE,),
        [pltpu.VMEM((pieces, depth, cols), BF), pltpu.SemaphoreType.DMA((pieces,))],
        8,
        2 * rows * cols * wide,
        rows * cols * 2,
        marks,
    )


def masked(slot, rank, count, lhs_ref):
    for m in range(count):
        lhs_ref[m * R : (m + 1) * R, :] = jnp.where(slot == m, rank, 0.0).astype(BF)


def tile_copies(wide_ref, held, sems, start):
    pieces, depth, width = held.shape
    copies = [
        pltpu.make_async_copy(
            wide_ref.at[pl.ds(p * depth, depth), pl.ds(start, width)], held.at[p], sems.at[p]
        )
        for p in range(pieces)
    ]
    for copy in copies:
        copy.start()
    return copies


def tile_dot(lhs_ref, held, copies):
    pieces, depth, width = held.shape
    total = jnp.zeros((lhs_ref.shape[0], width), F32)
    for p in range(pieces):
        copies[p].wait()
        total += jnp.dot(
            lhs_ref[:, p * depth : (p + 1) * depth], held[p], preferred_element_type=F32
        )
    return total.astype(BF)


def tile_scratch(rows, width, pieces=4):
    return [pltpu.VMEM((pieces, rows // pieces, width), BF), pltpu.SemaphoreType.DMA((pieces,))]


def first_call(flags, slot_rows, mine, theirs, acts, count, width, marks):
    rows = acts.shape[0]
    half = rows // 2

    def body(flag_ref, slot_ref, mine_ref, theirs_ref, acts_ref, out, lhs, d_own, d_half, held, sems):
        copies = tile_copies(acts_ref, held, sems, 0)
        rank = mine_ref[...] + theirs_ref[...]
        d_own[...] = rank.astype(BF)
        odd = flag_ref[ODD] == 1
        d_half[...] = jnp.where(odd, rank[:, half:], rank[:, :half]).astype(BF)
        masked(slot_ref[...], rank, count, lhs)
        out[...] = tile_dot(lhs, held, copies)

    return launch(
        body,
        (flags, slot_rows, mine, theirs, acts),
        (SCALARS, WHOLE, WHOLE, WHOLE, FAR),
        [
            jax.ShapeDtypeStruct((count * R, width), BF),
            jax.ShapeDtypeStruct((count * R, rows), BF),
            jax.ShapeDtypeStruct((R, rows), BF),
            jax.ShapeDtypeStruct((R, half), BF),
        ],
        [WHOLE] * 4,
        tile_scratch(rows, width),
        10,
        2 * rows * count * R * width,
        rows * width * 2,
        marks,
    )


def tiles_call(lhs, acts, tiles, marks):
    rows = acts.shape[0]
    n = len(tiles)
    total = sum(width for _, width in tiles)

    def body(lhs_ref, acts_ref, *refs):
        held, sems = refs[n::2], refs[n + 1 :: 2]
        copies = [
            tile_copies(acts_ref, held[i], sems[i], start) for i, (start, _) in enumerate(tiles)
        ]
        for i in range(n):
            refs[i][...] = tile_dot(lhs_ref, held[i], copies[i])

    return launch(
        body,
        (lhs, acts),
        (WHOLE, FAR),
        [jax.ShapeDtypeStruct((lhs.shape[0], width), BF) for _, width in tiles],
        [WHOLE] * n,
        [x for _, width in tiles for x in tile_scratch(rows, width)],
        12,
        2 * rows * lhs.shape[0] * total,
        rows * total * 2,
        marks,
    )


def place_call(position, firsts, seconds, start, total_rows, held):
    width = sum(part[2] for part in firsts)
    count = len(seconds[0][0])
    flat, reads = [], []
    for parts in (firsts, seconds):
        reads.append([])
        for arrays, offset, wide in parts:
            listed = isinstance(arrays, list)
            reads[-1].append((len(flat), listed, offset, wide))
            flat += arrays if listed else [arrays]
    extra = [] if held is None else [held]

    def kernel(flag_ref, *refs):
        out_ref, turned, sems = refs[-3:]

        def read(parts, m, here):
            got = []
            for k, listed, offset, wide in parts:
                cols = slice(offset, offset + wide)
                got.append(refs[k + m][:, cols] if listed else refs[k][here, cols])
            return jnp.concatenate(got, axis=1).astype(F32)

        copies = []
        for m in range(count):
            sender = jnp.bitwise_xor(flag_ref[PLACE], m)
            swapped = sender >= count // 2
            here = pl.ds(pl.multiple_of(sender * R, R), R)
            a, b = read(reads[0], m, here), read(reads[1], m, here)
            turned[m, :, :] = jnp.concatenate(
                [jnp.where(swapped, b, a), jnp.where(swapped, a, b)], axis=0
            ).T.astype(BF)
            row = pl.multiple_of(sender * (total_rows // count) + start, 128)
            copies.append(
                pltpu.make_async_copy(
                    turned.at[m], out_ref.at[pl.ds(row, width), :], sems.at[m]
                )
            )
            copies[-1].start()
        for copy in copies:
            copy.wait()

    return pl.pallas_call(
        kernel,
        out_shape=jax.ShapeDtypeStruct((total_rows, 2 * R), BF),
        in_specs=[SCALARS]
        + [WHOLE] * len(flat)
        + [pl.BlockSpec(memory_space=pl.ANY)] * len(extra),
        out_specs=pl.BlockSpec(memory_space=pl.ANY),
        scratch_shapes=[
            pltpu.VMEM((count, width, 2 * R), BF),
            pltpu.SemaphoreType.DMA((count,)),
        ],
        input_output_aliases={} if held is None else {1 + len(flat): 0},
        compiler_params=pltpu.CompilerParams(vmem_limit_bytes=12 * 1024 * 1024),
        cost_estimate=pl.CostEstimate(
            flops=1, bytes_accessed=4 * count * width * 2 * R * 2, transcendentals=0
        ),
    )(position, *flat, *extra)


def fold_call(pieces, groups, rows, marks):
    width = pieces.shape[1]
    per = pieces.shape[0] // groups // rows

    def body(in_ref, out_ref):
        for a in range(groups):
            total = jnp.zeros((rows, width), F32)
            for z in range(per):
                start = (a * per + z) * rows
                total += in_ref[start : start + rows, :].astype(F32)
            out_ref[:, a * width : (a + 1) * width] = total.astype(BF)

    return launch(
        body,
        (pieces,),
        (WHOLE,),
        [jax.ShapeDtypeStruct((rows, groups * width), BF)],
        [WHOLE],
        [],
        6,
        1,
        pieces.size * 3,
        marks,
    )[0]


def stack_call(flags, parts):
    rows, width = parts[0].shape

    def body(flag_ref, *refs):
        for m in range(len(parts)):
            place = jnp.bitwise_xor(flag_ref[DP_PLACE], m)
            refs[-1][pl.ds(pl.multiple_of(place * rows, rows), rows), :] = refs[m][...]

    return launch(
        body,
        (flags, *parts),
        (SCALARS, *[WHOLE] * len(parts)),
        [jax.ShapeDtypeStruct((rows * len(parts), width), BF)],
        [WHOLE],
        [],
        6,
        1,
        rows * width * 16,
        [],
    )[0]


def step_call(flags, arrays, outs, marks, count, start=None):
    names = list(arrays)
    out_names = list(outs)
    rows = None
    scratch = []
    mib = 4
    if start is not None:
        wide = arrays[WIDE]
        rows = wide.shape[0]
        width = outs[PART][1]
        scratch += tile_scratch(rows, width)
        scratch.append(pltpu.VMEM((count * R, rows), BF))
        mib += 7

    def body(flag_ref, *refs):
        got = dict(zip(names, refs[: len(names)]))
        put = dict(zip(out_names, refs[len(names) :]))
        rest = list(refs[len(names) + len(out_names) :])
        edge = flag_ref[EDGE] == 1
        inside = jnp.logical_not(edge)

        def add(a, b):
            return (got[a][...].astype(F32) + got[b][...].astype(F32)).astype(BF)

        if start is not None:
            held, sems = rest[:2]
            rest = rest[2:]
            copies = tile_copies(got[WIDE], held, sems, start)
        if INNER in put:
            put[INNER][...] = add(OLD_PART, FROM_LINE)
        if FINAL in put or (FINAL, 0) in put or FINALS in put:

            def finish(src):
                if FINAL in put:
                    put[FINAL][...] = src[...]
                elif FINALS in put:
                    first_width = got[OLD_FINAL].shape[1]
                    put[FINALS][:, :first_width] = got[OLD_FINAL][...]
                    put[FINALS][:, first_width:] = src[...]
                else:
                    for m in range(count):
                        place = jnp.bitwise_xor(flag_ref[PLACE], m)
                        here = pl.ds(pl.multiple_of(place * R, R), R)
                        first_width = 0
                        if OLD_FINAL in got:
                            first_width = got[OLD_FINAL].shape[1]
                            put[(FINAL, m)][:, :first_width] = got[OLD_FINAL][here, :]
                        put[(FINAL, m)][:, first_width:] = src[here, :]

            pl.when(edge)(lambda: finish(got[FROM_LINE]))
            pl.when(inside)(lambda: finish(got[OLD_LINE]))
        if KEEP in put:
            upper = flag_ref[UPPER] == 1
            key = got[SHRUNK_MINE][:R] + got[SHRUNK_THEIRS][:R]
            value = got[SHRUNK_MINE][R:] + got[SHRUNK_THEIRS][R:]
            put[KEEP][...] = jnp.where(upper, value, key)
            put[SEND][...] = jnp.where(upper, key, value).astype(BF)
        if start is not None:
            lhs = rest[0]
            if HALF_MINE in got:
                odd = flag_ref[ODD] == 1
                a, b = got[HALF_MINE][...].astype(F32), got[HALF_THEIRS][...].astype(F32)
                rank = jnp.concatenate([jnp.where(odd, b, a), jnp.where(odd, a, b)], axis=1)
                put[D_OTHER][...] = rank.astype(BF)
            elif KEPT in got:
                rank = got[KEPT][...] + got[CAME][...].astype(F32)
            else:
                rank = got[RANK][...].astype(F32)
            masked(got[SLOT_ROWS][...], rank, count, lhs)
            put[PART][...] = tile_dot(lhs, held, copies)
        if LINE in put:
            if OLD_INNER in got and (PART in got or start is not None):
                part = got[PART] if PART in got else put[PART]

                @pl.when(edge)
                def _():
                    put[LINE][...] = part[...]

                @pl.when(inside)
                def _():
                    put[LINE][...] = add(OLD_INNER, FROM_INNER)

            elif OLD_INNER in got:
                put[LINE][...] = add(OLD_INNER, FROM_INNER)
            else:
                put[LINE][...] = got.get(PART, put.get(PART))[...]
    made = launch(
        body,
        (flags, *arrays.values()),
        (SCALARS, *[FAR if k == WIDE else WHOLE for k in names]),
        [
            jax.ShapeDtypeStruct(shape, F32 if k == KEEP else BF)
            for k, shape in outs.items()
        ],
        [WHOLE] * len(outs),
        scratch,
        mib,
        15 * 10**9 if FROM_LINE in names else 1,
        24 * 10**6,
        marks,
    )
    return dict(zip([*out_names, MARK], made))


def shrink_call(slot, pool, acts, marks, per=4):
    rows, width = acts.shape

    def body(slot_ref, pool_ref, acts_ref, out_ref):
        i = pl.program_id(0)
        for b in range(per):
            here = slice(b * BLOCK, (b + 1) * BLOCK)
            part = jnp.dot(
                acts_ref[here, :], pool_ref[slot_ref[i * per + b]], preferred_element_type=F32
            )
            out_ref[:, here] = part.T

    return launch(
        body,
        (slot, pool, acts),
        (SCALARS, WHOLE, pl.BlockSpec((per * BLOCK, width), lambda i: (i, 0))),
        (jax.ShapeDtypeStruct((2 * R, rows), F32),),
        (pl.BlockSpec((2 * R, per * BLOCK), lambda i: (0, i)),),
        [],
        12,
        4 * rows * width * 2 * R,
        rows * width * 2,
        marks,
        (rows // (BLOCK * per),),
    )


def expand_call(flags, slot, pools, own, other, width, marks, per=4):
    rows = own.shape[1]

    def body(flag_ref, slot_ref, *refs):
        pool_refs = refs[: len(pools)]
        own_ref, other_ref, out_ref = refs[len(pools) :]
        i = pl.program_id(0)
        upper = flag_ref[UPPER] == 1
        for b in range(per):
            here = slice(b * BLOCK, (b + 1) * BLOCK)
            mine, theirs = own_ref[:, here].astype(F32), other_ref[:, here].astype(F32)
            rank = jnp.concatenate(
                [jnp.where(upper, theirs, mine), jnp.where(upper, mine, theirs)], axis=0
            )
            turned = rank.T.astype(BF)
            first = 0
            for pool_ref in pool_refs:
                depth = pool_ref.shape[1]
                out_ref[here, first : first + depth] = lax.dot_general(
                    turned,
                    pool_ref[slot_ref[i * per + b]],
                    (((1,), (1,)), ((), ())),
                    preferred_element_type=F32,
                ).astype(BF)
                first += depth

    return launch(
        body,
        (flags, slot, *pools, own, other),
        (
            SCALARS,
            SCALARS,
            *[WHOLE] * len(pools),
            pl.BlockSpec((R, per * BLOCK), lambda i: (0, i)),
            pl.BlockSpec((R, per * BLOCK), lambda i: (0, i)),
        ),
        (pltpu.HBM((rows, width), BF),),
        (pl.BlockSpec((per * BLOCK, width), lambda i: (i, 0)),),
        [],
        12,
        4 * rows * width * 2 * R,
        rows * width * 2,
        marks,
        (rows // (BLOCK * per),),
    )


def local(acts, out_grad, tenant_ids, slot_map, down_pool, up_pool):
    acts = pltpu.with_memory_space_constraint(acts, pltpu.HBM)
    out_grad = pltpu.with_memory_space_constraint(out_grad, pltpu.HBM)
    count = lax.axis_size("adapter")
    j = lax.axis_index("adapter")
    z = lax.axis_index("dp")
    rows, width = acts.shape
    cols = out_grad.shape[1]
    total_rows = down_pool.shape[1]
    edge = (z == 0) | (z == 3)
    flags = jnp.stack([edge.astype(jnp.int32), j // (count // 2), j % 2, j, z]).astype(jnp.int32)

    def swap(x, m):
        return lax.ppermute(x, "adapter", [(i, i ^ m) for i in range(count)])

    def to_owner(x):
        return lax.all_to_all(x, "adapter", split_axis=0, concat_axis=0, tiled=True)

    slot = slot_map[tenant_ids[:, 0]].astype(jnp.int32)
    slot_rows = jnp.repeat(slot, BLOCK)[None, :]

    def up_piece(m):
        return lax.dynamic_slice(up_pool[0], (0, (j ^ m) * cols), (R, cols))

    ups = [up_piece(0)] + [swap(up_piece(m), m) for m in range(1, count)]
    back_part, mark = back_call(flags, slot_rows, jnp.concatenate(ups, axis=0), out_grad, [])
    back_peer = swap(back_part, 1)

    unit = width // 16
    sizes = [5 * unit, 5 * unit, 6 * unit, 6 * unit, 5 * unit, 5 * unit]
    n = len(sizes)
    per_kind = n // 2
    starts = [sum(sizes[:c]) % width for c in range(n)]
    tenants = count * R
    parts, line, inner, from_line, from_inner, final = {}, {}, {}, {}, {}, {}
    parts[0], lhs_own, d_own, d_half, mark = first_call(
        flags, slot_rows, back_part, back_peer, acts, count, sizes[0], []
    )
    came_half = swap(d_half, 2)
    came_other = swap(came_half, 1)
    tiles = [(starts[c], sizes[c]) for c in range(1, per_kind)]
    *more, mark = tiles_call(lhs_own, acts, tiles, [mark])
    for c in range(1, per_kind):
        parts[c] = more[c - 1]

    for t in range(n + 6):
        if t < 2:
            line[t] = parts[t]
        else:
            arrays, outs, start = {}, {}, None
            if t < n and t in parts:
                arrays[PART] = parts[t]
            elif t < n:
                start = starts[t]
                arrays[WIDE], arrays[SLOT_ROWS] = acts, slot_rows
                outs[PART] = (tenants, sizes[t])
                if t == per_kind:
                    arrays[HALF_MINE], arrays[HALF_THEIRS] = came_half, came_other
                    outs[D_OTHER] = (R, rows)
                else:
                    arrays[RANK] = d_other
            arrays[FROM_LINE] = from_line[t - 2]
            if t - 2 < n:
                arrays[OLD_PART] = parts[t - 2]
                outs[INNER] = (tenants, sizes[t - 2])
            if 0 <= t - 4 < n:
                arrays[OLD_INNER] = inner[t - 2]
                arrays[FROM_INNER] = from_inner[t - 2]
            if t < n or 0 <= t - 4 < n:
                outs[LINE] = (tenants, sizes[t] if t < n else sizes[t - 4])
            if t >= 6:
                arrays[OLD_LINE] = line[t - 2]
                c = t - 6
                if c in (0, per_kind - 1):
                    outs[FINAL] = (tenants, sizes[c])
                elif c == n - 1:
                    outs.update({(FINAL, m): (R, sizes[c]) for m in range(count)})
                else:
                    arrays[OLD_FINAL] = final[c - 1]
                    wide_now = final[c - 1].shape[1] + sizes[c]
                    if c == n - 2:
                        outs.update({(FINAL, m): (R, wide_now) for m in range(count)})
                    else:
                        outs[FINALS] = (tenants, wide_now)
            if t == 8:
                arrays[SHRUNK_MINE], arrays[SHRUNK_THEIRS] = shrunk_part, swap(shrunk_part, 1)
                outs[KEEP] = outs[SEND] = (R, rows)
            marks = [mark]
            if t == 10:
                late = {WIDE: out_grad, KEPT: keep, CAME: came_shrunk, SLOT_ROWS: slot_rows}
                made = step_call(flags, late, {PART: (tenants, cols)}, [mark], count, 0)
                up, mark = made[PART], made[MARK]
                marks = [mark, own]
                up_pieces = lax.all_to_all(
                    up, ("adapter", "dp"), split_axis=0, concat_axis=0, tiled=True
                )
            if t == 6:
                shrunk_part, mark = shrink_call(slot, pools[0], acts, [mark])
                marks = [mark]
            made = step_call(flags, arrays, outs, marks, count, start)
            mark = made[MARK]
            if t == 2:
                pool_in, _ = lax.optimization_barrier((down_pool[0], mark))
                pool = to_owner(pool_in).reshape(count, width, 2 * R)
                pools = [pltpu.with_memory_space_constraint(pool, pltpu.HBM)]
            if PART in made and t < n:
                parts[t] = made[PART]
            if t == per_kind:
                d_other = made[D_OTHER]
            if INNER in made:
                inner[t] = made[INNER]
            if LINE in made:
                line[t] = made[LINE]
            if FINAL in made:
                final[t - 6] = made[FINAL]
            if FINALS in made:
                final[t - 6] = made[FINALS]
            if t == 7:
                own = to_owner(made[FINALS])
            if (FINAL, 0) in made:
                final[t - 6] = [made[(FINAL, 0)]] + [
                    swap(made[(FINAL, m)], m) for m in range(1, count)
                ]
            if t == 8:
                keep, came_shrunk = made[KEEP], swap(made[SEND], 2)
        if t in line and t < n + 4:
            from_line[t] = lax.ppermute(line[t], "dp", [(0, 1), (1, 0), (2, 3), (3, 2)])
        if t in inner:
            from_inner[t] = lax.ppermute(inner[t], "dp", [(1, 2), (2, 1)])

    acts_grad, mark = expand_call(flags, slot, pools, d_own, d_other, width, [mark])
    dp = lax.axis_size("dp")
    up_rows = fold_call(up_pieces, count, R // dp, [mark])
    up_parts = [up_rows] + [
        lax.ppermute(up_rows, "dp", [(i, i ^ m) for i in range(dp)]) for m in range(1, dp)
    ]
    up_grad = stack_call(flags, up_parts)
    down_grad = None
    mixed, last = final[n - 2], final[n - 1]
    joint, rest, split = sizes[0] + sizes[1], sizes[2], width - sizes[n - 1]
    down_grad = place_call(
        flags,
        [(own, 0, joint), (mixed, 0, split - joint)],
        [(mixed, rest, split)],
        0,
        total_rows,
        None,
    )
    down_grad = place_call(
        flags,
        [(mixed, split - joint, width - split)],
        [(last, 0, width - split)],
        split,
        total_rows,
        down_grad,
    )
    return acts_grad, down_grad[None], up_grad[None]


def local_any(acts, out_grad, tenant_ids, slot_map, down_pool, up_pool):
    position = lax.axis_index("adapter")
    row_count, local_width = acts.shape
    col_count = out_grad.shape[1]
    block_count = row_count // BLOCK
    tenant_slot = slot_map[tenant_ids[:, 0]]
    down_slices = lax.all_to_all(down_pool, "adapter", split_axis=1, concat_axis=0, tiled=True)
    up_slices = lax.all_to_all(up_pool, "adapter", split_axis=2, concat_axis=0, tiled=True)
    tenant_count = down_slices.shape[0]
    acts_blocks = acts.reshape(block_count, BLOCK, local_width)
    grad_blocks = out_grad.reshape(block_count, BLOCK, col_count)
    down_blocks = down_slices[tenant_slot]
    up_blocks = up_slices[tenant_slot]
    shrunk_part = jnp.einsum(
        "bnd,bdr->bnr", acts_blocks, down_blocks, preferred_element_type=jnp.float32
    )
    back_part = jnp.einsum(
        "bnc,brc->bnr", grad_blocks, up_blocks, preferred_element_type=jnp.float32
    )
    is_key = position * col_count < DKV
    zero_part = jnp.zeros_like(back_part)
    d_part = jnp.where(
        is_key,
        jnp.concatenate([back_part, zero_part], axis=-1),
        jnp.concatenate([zero_part, back_part], axis=-1),
    )
    shrunk_sum, d_sum = lax.psum((shrunk_part, d_part), "adapter")
    shrunk = shrunk_sum.astype(jnp.bfloat16)
    d_shrunk = d_sum.astype(jnp.bfloat16)
    acts_grad = jnp.einsum(
        "bnr,bdr->bnd", d_shrunk, down_blocks, preferred_element_type=jnp.float32
    )
    acts_grad = acts_grad.astype(jnp.bfloat16).reshape(row_count, local_width)
    part_down = jnp.einsum(
        "bnd,bnr->bdr", acts_blocks, d_shrunk, preferred_element_type=jnp.float32
    )
    own_shrunk = jnp.where(is_key, shrunk[..., :R], shrunk[..., R:])
    part_up = jnp.einsum(
        "bnr,bnc->brc", own_shrunk, grad_blocks, preferred_element_type=jnp.float32
    )
    member = (tenant_slot[None, :] == jnp.arange(tenant_count, dtype=jnp.int32)[:, None]).astype(
        jnp.float32
    )
    grad_down = jnp.einsum("tb,bdr->tdr", member, part_down, precision=lax.Precision.HIGHEST)
    grad_up = jnp.einsum("tb,brc->trc", member, part_up, precision=lax.Precision.HIGHEST)
    owned_down = lax.all_to_all(grad_down, "adapter", split_axis=0, concat_axis=1, tiled=True)
    owned_up = lax.all_to_all(grad_up, "adapter", split_axis=0, concat_axis=2, tiled=True)
    total_down, total_up = lax.psum((owned_down, owned_up), "dp")
    down_grad = total_down.astype(jnp.bfloat16)
    up_grad = total_up.astype(jnp.bfloat16)
    return (acts_grad, down_grad, up_grad)


def solution(mesh):
    line_of_four = mesh.shape["adapter"] == 4 and mesh.shape["dp"] == 4
    return jax.shard_map(
        local if line_of_four else local_any,
        mesh=mesh,
        in_specs=(
            P(("groups", "dp"), "adapter"),
            P(("groups", "dp"), "adapter"),
            P(("groups", "dp"), None),
            P("groups"),
            P(("groups", "adapter"), None, None),
            P(("groups", "adapter"), None, None),
        ),
        out_specs=(
            P(("groups", "dp"), "adapter"),
            P(("groups", "adapter"), None, None),
            P(("groups", "adapter"), None, None),
        ),
        check_vma=False,
    )
```

```python
import jax
import jax.numpy as jnp
from jax import lax
from jax.experimental import pallas as pl
from jax.experimental.pallas import tpu as pltpu
from jax.sharding import PartitionSpec as P

DKV = 1024
R = 64
BLOCK = 128
BF = jnp.bfloat16
F32 = jnp.float32
WHOLE = pl.BlockSpec(memory_space=pltpu.VMEM)
SCALARS = pl.BlockSpec(memory_space=pltpu.SMEM)
FAR = pl.BlockSpec(memory_space=pltpu.HBM)
EDGE, UPPER, ODD, PLACE, DP_PLACE = range(5)
(
    PART, FROM_LINE, OLD_PART, INNER, OLD_INNER, FROM_INNER, LINE, OLD_LINE, FINAL, FINALS,
    OLD_FINAL, WIDE, KEEP, SEND, SHRUNK_MINE, SHRUNK_THEIRS, KEPT, CAME, SLOT_ROWS,
    HALF_MINE, HALF_THEIRS, D_OTHER, RANK, MARK,
) = range(24)


def launch(body, args, specs, outs, out_specs, scratch, mib, flops, moved, marks, grid=()):
    n_in, n_args, n_outs = len(args) + len(marks), len(args), len(outs)

    def kernel(*refs):
        refs[n_in + n_outs][...] = jnp.zeros((8, 128), F32)
        body(*refs[:n_args], *refs[n_in : n_in + n_outs], *refs[n_in + n_outs + 1 :])

    return pl.pallas_call(
        kernel,
        grid=grid,
        out_shape=[*outs, jax.ShapeDtypeStruct((8, 128), F32)],
        in_specs=[*specs, *[pl.BlockSpec(memory_space=pl.ANY)] * len(marks)],
        out_specs=[*out_specs, WHOLE],
        scratch_shapes=scratch,
        compiler_params=pltpu.CompilerParams(vmem_limit_bytes=mib * 1024 * 1024),
        cost_estimate=pl.CostEstimate(flops=flops, bytes_accessed=moved, transcendentals=0),
    )(*args, *marks)


def back_call(flags, slot_rows, up_stack, out_grad, marks, pieces=4):
    rows, cols = out_grad.shape
    wide = up_stack.shape[0]
    depth = rows // pieces

    def body(flag_ref, slot_ref, up_ref, grad_ref, out_ref, held, sems):
        copies = []
        for p in range(pieces):
            here = pl.ds(p * depth, depth)
            copies.append(pltpu.make_async_copy(grad_ref.at[here, :], held.at[p], sems.at[p]))
            copies[-1].start()
        for p in range(pieces):
            copies[p].wait()
            here = slice(p * depth, (p + 1) * depth)
            every = lax.dot_general(
                up_ref[...], held[p], (((1,), (1,)), ((), ())), preferred_element_type=F32
            )
            rel = jnp.bitwise_xor(slot_ref[:, here], flag_ref[PLACE])
            total = jnp.zeros((R, depth), F32)
            for m in range(wide // R):
                total += jnp.where(rel == m, every[m * R : (m + 1) * R], 0.0)
            out_ref[:, here] = total

    return launch(
        body,
        (flags, slot_rows, up_stack, out_grad),
        (SCALARS, WHOLE, WHOLE, FAR),
        (jax.ShapeDtypeStruct((R, rows), F32),),
        (WHOLE,),
        [pltpu.VMEM((pieces, depth, cols), BF), pltpu.SemaphoreType.DMA((pieces,))],
        8,
        2 * rows * cols * wide,
        rows * cols * 2,
        marks,
    )


def masked(slot, rank, count, lhs_ref):
    for m in range(count):
        lhs_ref[m * R : (m + 1) * R, :] = jnp.where(slot == m, rank, 0.0).astype(BF)


def tile_copies(wide_ref, held, sems, start):
    pieces, depth, width = held.shape
    copies = [
        pltpu.make_async_copy(
            wide_ref.at[pl.ds(p * depth, depth), pl.ds(start, width)], held.at[p], sems.at[p]
        )
        for p in range(pieces)
    ]
    for copy in copies:
        copy.start()
    return copies


def tile_dot(lhs_ref, held, copies):
    pieces, depth, width = held.shape
    total = jnp.zeros((lhs_ref.shape[0], width), F32)
    for p in range(pieces):
        copies[p].wait()
        total += jnp.dot(
            lhs_ref[:, p * depth : (p + 1) * depth], held[p], preferred_element_type=F32
        )
    return total.astype(BF)


def tile_scratch(rows, width, pieces=4):
    return [pltpu.VMEM((pieces, rows // pieces, width), BF), pltpu.SemaphoreType.DMA((pieces,))]


def first_call(flags, slot_rows, mine, theirs, acts, count, width, marks):
    rows = acts.shape[0]
    half = rows // 2

    def body(flag_ref, slot_ref, mine_ref, theirs_ref, acts_ref, out, lhs, d_own, d_half, held, sems):
        copies = tile_copies(acts_ref, held, sems, 0)
        rank = mine_ref[...] + theirs_ref[...]
        d_own[...] = rank.astype(BF)
        odd = flag_ref[ODD] == 1
        d_half[...] = jnp.where(odd, rank[:, half:], rank[:, :half]).astype(BF)
        masked(slot_ref[...], rank, count, lhs)
        out[...] = tile_dot(lhs, held, copies)

    return launch(
        body,
        (flags, slot_rows, mine, theirs, acts),
        (SCALARS, WHOLE, WHOLE, WHOLE, FAR),
        [
            jax.ShapeDtypeStruct((count * R, width), BF),
            jax.ShapeDtypeStruct((count * R, rows), BF),
            jax.ShapeDtypeStruct((R, rows), BF),
            jax.ShapeDtypeStruct((R, half), BF),
        ],
        [WHOLE] * 4,
        tile_scratch(rows, width),
        10,
        2 * rows * count * R * width,
        rows * width * 2,
        marks,
    )


def tiles_call(lhs, acts, tiles, marks):
    rows = acts.shape[0]
    n = len(tiles)
    total = sum(width for _, width in tiles)

    def body(lhs_ref, acts_ref, *refs):
        held, sems = refs[n::2], refs[n + 1 :: 2]
        copies = [
            tile_copies(acts_ref, held[i], sems[i], start) for i, (start, _) in enumerate(tiles)
        ]
        for i in range(n):
            refs[i][...] = tile_dot(lhs_ref, held[i], copies[i])

    return launch(
        body,
        (lhs, acts),
        (WHOLE, FAR),
        [jax.ShapeDtypeStruct((lhs.shape[0], width), BF) for _, width in tiles],
        [WHOLE] * n,
        [x for _, width in tiles for x in tile_scratch(rows, width)],
        12,
        2 * rows * lhs.shape[0] * total,
        rows * total * 2,
        marks,
    )


def place_call(position, firsts, seconds, start, total_rows, held):
    width = sum(part[2] for part in firsts)
    count = len(seconds[0][0])
    flat, reads = [], []
    for parts in (firsts, seconds):
        reads.append([])
        for arrays, offset, wide in parts:
            listed = isinstance(arrays, list)
            reads[-1].append((len(flat), listed, offset, wide))
            flat += arrays if listed else [arrays]
    extra = [] if held is None else [held]

    def kernel(flag_ref, *refs):
        out_ref, turned, sems = refs[-3:]

        def read(parts, m, here):
            got = []
            for k, listed, offset, wide in parts:
                cols = slice(offset, offset + wide)
                got.append(refs[k + m][:, cols] if listed else refs[k][here, cols])
            return jnp.concatenate(got, axis=1).astype(F32)

        copies = []
        for m in range(count):
            sender = jnp.bitwise_xor(flag_ref[PLACE], m)
            swapped = sender >= count // 2
            here = pl.ds(pl.multiple_of(sender * R, R), R)
            a, b = read(reads[0], m, here), read(reads[1], m, here)
            turned[m, :, :] = jnp.concatenate(
                [jnp.where(swapped, b, a), jnp.where(swapped, a, b)], axis=0
            ).T.astype(BF)
            row = pl.multiple_of(sender * (total_rows // count) + start, 128)
            copies.append(
                pltpu.make_async_copy(
                    turned.at[m], out_ref.at[pl.ds(row, width), :], sems.at[m]
                )
            )
            copies[-1].start()
        for copy in copies:
            copy.wait()

    return pl.pallas_call(
        kernel,
        out_shape=jax.ShapeDtypeStruct((total_rows, 2 * R), BF),
        in_specs=[SCALARS]
        + [WHOLE] * len(flat)
        + [pl.BlockSpec(memory_space=pl.ANY)] * len(extra),
        out_specs=pl.BlockSpec(memory_space=pl.ANY),
        scratch_shapes=[
            pltpu.VMEM((count, width, 2 * R), BF),
            pltpu.SemaphoreType.DMA((count,)),
        ],
        input_output_aliases={} if held is None else {1 + len(flat): 0},
        compiler_params=pltpu.CompilerParams(vmem_limit_bytes=12 * 1024 * 1024),
        cost_estimate=pl.CostEstimate(
            flops=15 * 10**9, bytes_accessed=4 * count * width * 2 * R * 2, transcendentals=0
        ),
    )(position, *flat, *extra)


def fold_call(pieces, groups, rows, marks):
    width = pieces.shape[1]
    per = pieces.shape[0] // groups // rows

    def body(in_ref, out_ref):
        for a in range(groups):
            total = jnp.zeros((rows, width), F32)
            for z in range(per):
                start = (a * per + z) * rows
                total += in_ref[start : start + rows, :].astype(F32)
            out_ref[:, a * width : (a + 1) * width] = total.astype(BF)

    return launch(
        body,
        (pieces,),
        (WHOLE,),
        [jax.ShapeDtypeStruct((rows, groups * width), BF)],
        [WHOLE],
        [],
        6,
        1,
        pieces.size * 3,
        marks,
    )[0]


def stack_call(flags, parts):
    rows, width = parts[0].shape

    def body(flag_ref, *refs):
        for m in range(len(parts)):
            place = jnp.bitwise_xor(flag_ref[DP_PLACE], m)
            refs[-1][pl.ds(pl.multiple_of(place * rows, rows), rows), :] = refs[m][...]

    return launch(
        body,
        (flags, *parts),
        (SCALARS, *[WHOLE] * len(parts)),
        [jax.ShapeDtypeStruct((rows * len(parts), width), BF)],
        [WHOLE],
        [],
        6,
        1,
        rows * width * 16,
        [],
    )[0]


def step_call(flags, arrays, outs, marks, count, start=None):
    names = list(arrays)
    out_names = list(outs)
    rows = None
    scratch = []
    mib = 4
    if start is not None:
        wide = arrays[WIDE]
        rows = wide.shape[0]
        width = outs[PART][1]
        scratch += tile_scratch(rows, width)
        scratch.append(pltpu.VMEM((count * R, rows), BF))
        mib += 7

    def body(flag_ref, *refs):
        got = dict(zip(names, refs[: len(names)]))
        put = dict(zip(out_names, refs[len(names) :]))
        rest = list(refs[len(names) + len(out_names) :])
        edge = flag_ref[EDGE] == 1
        inside = jnp.logical_not(edge)

        def add(a, b):
            return (got[a][...].astype(F32) + got[b][...].astype(F32)).astype(BF)

        if start is not None:
            held, sems = rest[:2]
            rest = rest[2:]
            copies = tile_copies(got[WIDE], held, sems, start)
        if INNER in put:
            put[INNER][...] = add(OLD_PART, FROM_LINE)
        if FINAL in put or (FINAL, 0) in put or FINALS in put:

            def finish(src):
                if FINAL in put:
                    put[FINAL][...] = src[...]
                elif FINALS in put:
                    first_width = got[OLD_FINAL].shape[1]
                    put[FINALS][:, :first_width] = got[OLD_FINAL][...]
                    put[FINALS][:, first_width:] = src[...]
                else:
                    for m in range(count):
                        place = jnp.bitwise_xor(flag_ref[PLACE], m)
                        here = pl.ds(pl.multiple_of(place * R, R), R)
                        first_width = 0
                        if OLD_FINAL in got:
                            first_width = got[OLD_FINAL].shape[1]
                            put[(FINAL, m)][:, :first_width] = got[OLD_FINAL][here, :]
                        put[(FINAL, m)][:, first_width:] = src[here, :]

            pl.when(edge)(lambda: finish(got[FROM_LINE]))
            pl.when(inside)(lambda: finish(got[OLD_LINE]))
        if KEEP in put:
            upper = flag_ref[UPPER] == 1
            key = got[SHRUNK_MINE][:R] + got[SHRUNK_THEIRS][:R]
            value = got[SHRUNK_MINE][R:] + got[SHRUNK_THEIRS][R:]
            put[KEEP][...] = jnp.where(upper, value, key)
            put[SEND][...] = jnp.where(upper, key, value).astype(BF)
        if start is not None:
            lhs = rest[0]
            if HALF_MINE in got:
                odd = flag_ref[ODD] == 1
                a, b = got[HALF_MINE][...].astype(F32), got[HALF_THEIRS][...].astype(F32)
                rank = jnp.concatenate([jnp.where(odd, b, a), jnp.where(odd, a, b)], axis=1)
                put[D_OTHER][...] = rank.astype(BF)
            elif KEPT in got:
                rank = got[KEPT][...] + got[CAME][...].astype(F32)
            else:
                rank = got[RANK][...].astype(F32)
            masked(got[SLOT_ROWS][...], rank, count, lhs)
            put[PART][...] = tile_dot(lhs, held, copies)
        if LINE in put:
            if OLD_INNER in got and (PART in got or start is not None):
                part = got[PART] if PART in got else put[PART]

                @pl.when(edge)
                def _():
                    put[LINE][...] = part[...]

                @pl.when(inside)
                def _():
                    put[LINE][...] = add(OLD_INNER, FROM_INNER)

            elif OLD_INNER in got:
                put[LINE][...] = add(OLD_INNER, FROM_INNER)
            else:
                put[LINE][...] = got.get(PART, put.get(PART))[...]
    made = launch(
        body,
        (flags, *arrays.values()),
        (SCALARS, *[FAR if k == WIDE else WHOLE for k in names]),
        [
            jax.ShapeDtypeStruct(shape, F32 if k == KEEP else BF)
            for k, shape in outs.items()
        ],
        [WHOLE] * len(outs),
        scratch,
        mib,
        15 * 10**9 if FROM_LINE in names else 1,
        24 * 10**6,
        marks,
    )
    return dict(zip([*out_names, MARK], made))


def shrink_call(slot, pool, acts, marks, per=8):
    rows, width = acts.shape

    def body(slot_ref, pool_ref, acts_ref, out_ref):
        i = pl.program_id(0)
        for b in range(per):
            here = slice(b * BLOCK, (b + 1) * BLOCK)
            part = jnp.dot(
                acts_ref[here, :], pool_ref[slot_ref[i * per + b]], preferred_element_type=F32
            )
            out_ref[:, here] = part.T

    return launch(
        body,
        (slot, pool, acts),
        (SCALARS, WHOLE, pl.BlockSpec((per * BLOCK, width), lambda i: (i, 0))),
        (jax.ShapeDtypeStruct((2 * R, rows), F32),),
        (pl.BlockSpec((2 * R, per * BLOCK), lambda i: (0, i)),),
        [],
        16,
        4 * rows * width * 2 * R,
        rows * width * 2,
        marks,
        (rows // (BLOCK * per),),
    )


def expand_call(flags, slot, pools, own, other, width, marks, per=4):
    rows = own.shape[1]

    def body(flag_ref, slot_ref, *refs):
        pool_refs = refs[: len(pools)]
        own_ref, other_ref, out_ref = refs[len(pools) :]
        i = pl.program_id(0)
        upper = flag_ref[UPPER] == 1
        for b in range(per):
            here = slice(b * BLOCK, (b + 1) * BLOCK)
            mine, theirs = own_ref[:, here].astype(F32), other_ref[:, here].astype(F32)
            rank = jnp.concatenate(
                [jnp.where(upper, theirs, mine), jnp.where(upper, mine, theirs)], axis=0
            )
            turned = rank.T.astype(BF)
            first = 0
            for pool_ref in pool_refs:
                depth = pool_ref.shape[1]
                out_ref[here, first : first + depth] = lax.dot_general(
                    turned,
                    pool_ref[slot_ref[i * per + b]],
                    (((1,), (1,)), ((), ())),
                    preferred_element_type=F32,
                ).astype(BF)
                first += depth

    return launch(
        body,
        (flags, slot, *pools, own, other),
        (
            SCALARS,
            SCALARS,
            *[WHOLE] * len(pools),
            pl.BlockSpec((R, per * BLOCK), lambda i: (0, i)),
            pl.BlockSpec((R, per * BLOCK), lambda i: (0, i)),
        ),
        (pltpu.HBM((rows, width), BF),),
        (pl.BlockSpec((per * BLOCK, width), lambda i: (i, 0)),),
        [],
        12,
        4 * rows * width * 2 * R,
        rows * width * 2,
        marks,
        (rows // (BLOCK * per),),
    )


def local(acts, out_grad, tenant_ids, slot_map, down_pool, up_pool):
    acts = pltpu.with_memory_space_constraint(acts, pltpu.HBM)
    out_grad = pltpu.with_memory_space_constraint(out_grad, pltpu.HBM)
    count = lax.axis_size("adapter")
    j = lax.axis_index("adapter")
    z = lax.axis_index("dp")
    rows, width = acts.shape
    cols = out_grad.shape[1]
    total_rows = down_pool.shape[1]
    edge = (z == 0) | (z == 3)
    flags = jnp.stack([edge.astype(jnp.int32), j // (count // 2), j % 2, j, z]).astype(jnp.int32)

    def swap(x, m):
        return lax.ppermute(x, "adapter", [(i, i ^ m) for i in range(count)])

    def to_owner(x):
        return lax.all_to_all(x, "adapter", split_axis=0, concat_axis=0, tiled=True)

    slot = slot_map[tenant_ids[:, 0]].astype(jnp.int32)
    slot_rows = jnp.repeat(slot, BLOCK)[None, :]

    def up_piece(m):
        return lax.dynamic_slice(up_pool[0], (0, (j ^ m) * cols), (R, cols))

    ups = [up_piece(0)] + [swap(up_piece(m), m) for m in range(1, count)]
    back_part, mark = back_call(flags, slot_rows, jnp.concatenate(ups, axis=0), out_grad, [])
    back_peer = swap(back_part, 1)

    unit = width // 16
    sizes = [5 * unit, 5 * unit, 6 * unit, 6 * unit, 5 * unit, 5 * unit]
    n = len(sizes)
    per_kind = n // 2
    starts = [sum(sizes[:c]) % width for c in range(n)]
    tenants = count * R
    parts, line, inner, from_line, from_inner, final = {}, {}, {}, {}, {}, {}
    parts[0], lhs_own, d_own, d_half, mark = first_call(
        flags, slot_rows, back_part, back_peer, acts, count, sizes[0], []
    )
    came_half = swap(d_half, 2)
    came_other = swap(came_half, 1)
    tiles = [(starts[c], sizes[c]) for c in range(1, per_kind)]
    *more, mark = tiles_call(lhs_own, acts, tiles, [mark])
    for c in range(1, per_kind):
        parts[c] = more[c - 1]
    pool_in, _, _ = lax.optimization_barrier((down_pool[0], mark, came_half))
    pool = to_owner(pool_in).reshape(count, width, 2 * R)
    pools = [pltpu.with_memory_space_constraint(pool, pltpu.HBM)]

    for t in range(n + 6):
        if t < 2:
            line[t] = parts[t]
        else:
            arrays, outs, start = {}, {}, None
            if t < n and t in parts:
                arrays[PART] = parts[t]
            elif t < n:
                start = starts[t]
                arrays[WIDE], arrays[SLOT_ROWS] = acts, slot_rows
                outs[PART] = (tenants, sizes[t])
                if t == per_kind:
                    arrays[HALF_MINE], arrays[HALF_THEIRS] = came_half, came_other
                    outs[D_OTHER] = (R, rows)
                else:
                    arrays[RANK] = d_other
            arrays[FROM_LINE] = from_line[t - 2]
            if t - 2 < n:
                arrays[OLD_PART] = parts[t - 2]
                outs[INNER] = (tenants, sizes[t - 2])
            if 0 <= t - 4 < n:
                arrays[OLD_INNER] = inner[t - 2]
                arrays[FROM_INNER] = from_inner[t - 2]
            if t < n or 0 <= t - 4 < n:
                outs[LINE] = (tenants, sizes[t] if t < n else sizes[t - 4])
            if t >= 6:
                arrays[OLD_LINE] = line[t - 2]
                c = t - 6
                if c in (0, per_kind - 1, n - 2):
                    outs[FINAL] = (tenants, sizes[c])
                else:
                    arrays[OLD_FINAL] = final[c - 1]
                    wide_now = final[c - 1].shape[1] + sizes[c]
                    if c >= per_kind:
                        outs.update({(FINAL, m): (R, wide_now) for m in range(count)})
                    else:
                        outs[FINALS] = (tenants, wide_now)
            if t == 8:
                arrays[SHRUNK_MINE], arrays[SHRUNK_THEIRS] = shrunk_part, swap(shrunk_part, 1)
                outs[KEEP] = outs[SEND] = (R, rows)
            marks = [mark]
            if t == 10:
                late = {WIDE: out_grad, KEPT: keep, CAME: came_shrunk, SLOT_ROWS: slot_rows}
                made = step_call(flags, late, {PART: (tenants, cols)}, [mark], count, 0)
                up, mark = made[PART], made[MARK]
                marks = [mark, own]
                up_pieces = lax.all_to_all(
                    up, ("adapter", "dp"), split_axis=0, concat_axis=0, tiled=True
                )
            if t == 9:
                acts_grad, mark = expand_call(flags, slot, pools, d_own, d_other, width, [mark])
                marks = [mark]
            if t == 6:
                shrunk_part, mark = shrink_call(slot, pools[0], acts, [mark])
                marks = [mark]
            made = step_call(flags, arrays, outs, marks, count, start)
            mark = made[MARK]
            if PART in made and t < n:
                parts[t] = made[PART]
            if t == per_kind:
                d_other = made[D_OTHER]
            if INNER in made:
                inner[t] = made[INNER]
            if LINE in made:
                line[t] = made[LINE]
            if FINAL in made:
                final[t - 6] = made[FINAL]
            if FINALS in made:
                final[t - 6] = made[FINALS]
            if t == 7:
                own = to_owner(made[FINALS])
            if (FINAL, 0) in made:
                final[t - 6] = [made[(FINAL, 0)]] + [
                    swap(made[(FINAL, m)], m) for m in range(1, count)
                ]
            if t == 8:
                keep, came_shrunk = made[KEEP], swap(made[SEND], 2)
        if t in line and t < n + 4:
            from_line[t] = lax.ppermute(line[t], "dp", [(0, 1), (1, 0), (2, 3), (3, 2)])
        if t in inner:
            from_inner[t] = lax.ppermute(inner[t], "dp", [(1, 2), (2, 1)])

    dp = lax.axis_size("dp")
    up_rows = fold_call(up_pieces, count, R // dp, [mark])
    up_parts = [up_rows] + [
        lax.ppermute(up_rows, "dp", [(i, i ^ m) for i in range(dp)]) for m in range(1, dp)
    ]
    up_grad = stack_call(flags, up_parts)
    down_grad = None
    mixed, last = final[per_kind], final[n - 1]
    joint, split = sizes[0] + sizes[1], sizes[per_kind]
    down_grad = place_call(
        flags, [(own, 0, split)], [(mixed, width - joint, split)], 0, total_rows, None
    )
    down_grad = place_call(
        flags,
        [(own, split, joint - split), (mixed, 0, width - joint)],
        [(last, 0, width - split)],
        split,
        total_rows,
        down_grad,
    )
    return acts_grad, down_grad[None], up_grad[None]


def local_any(acts, out_grad, tenant_ids, slot_map, down_pool, up_pool):
    position = lax.axis_index("adapter")
    row_count, local_width = acts.shape
    col_count = out_grad.shape[1]
    block_count = row_count // BLOCK
    tenant_slot = slot_map[tenant_ids[:, 0]]
    down_slices = lax.all_to_all(down_pool, "adapter", split_axis=1, concat_axis=0, tiled=True)
    up_slices = lax.all_to_all(up_pool, "adapter", split_axis=2, concat_axis=0, tiled=True)
    tenant_count = down_slices.shape[0]
    acts_blocks = acts.reshape(block_count, BLOCK, local_width)
    grad_blocks = out_grad.reshape(block_count, BLOCK, col_count)
    down_blocks = down_slices[tenant_slot]
    up_blocks = up_slices[tenant_slot]
    shrunk_part = jnp.einsum(
        "bnd,bdr->bnr", acts_blocks, down_blocks, preferred_element_type=jnp.float32
    )
    back_part = jnp.einsum(
        "bnc,brc->bnr", grad_blocks, up_blocks, preferred_element_type=jnp.float32
    )
    is_key = position * col_count < DKV
    zero_part = jnp.zeros_like(back_part)
    d_part = jnp.where(
        is_key,
        jnp.concatenate([back_part, zero_part], axis=-1),
        jnp.concatenate([zero_part, back_part], axis=-1),
    )
    shrunk_sum, d_sum = lax.psum((shrunk_part, d_part), "adapter")
    shrunk = shrunk_sum.astype(jnp.bfloat16)
    d_shrunk = d_sum.astype(jnp.bfloat16)
    acts_grad = jnp.einsum(
        "bnr,bdr->bnd", d_shrunk, down_blocks, preferred_element_type=jnp.float32
    )
    acts_grad = acts_grad.astype(jnp.bfloat16).reshape(row_count, local_width)
    part_down = jnp.einsum(
        "bnd,bnr->bdr", acts_blocks, d_shrunk, preferred_element_type=jnp.float32
    )
    own_shrunk = jnp.where(is_key, shrunk[..., :R], shrunk[..., R:])
    part_up = jnp.einsum(
        "bnr,bnc->brc", own_shrunk, grad_blocks, preferred_element_type=jnp.float32
    )
    member = (tenant_slot[None, :] == jnp.arange(tenant_count, dtype=jnp.int32)[:, None]).astype(
        jnp.float32
    )
    grad_down = jnp.einsum("tb,bdr->tdr", member, part_down, precision=lax.Precision.HIGHEST)
    grad_up = jnp.einsum("tb,brc->trc", member, part_up, precision=lax.Precision.HIGHEST)
    owned_down = lax.all_to_all(grad_down, "adapter", split_axis=0, concat_axis=1, tiled=True)
    owned_up = lax.all_to_all(grad_up, "adapter", split_axis=0, concat_axis=2, tiled=True)
    total_down, total_up = lax.psum((owned_down, owned_up), "dp")
    down_grad = total_down.astype(jnp.bfloat16)
    up_grad = total_up.astype(jnp.bfloat16)
    return (acts_grad, down_grad, up_grad)


def solution(mesh):
    line_of_four = mesh.shape["adapter"] == 4 and mesh.shape["dp"] == 4
    return jax.shard_map(
        local if line_of_four else local_any,
        mesh=mesh,
        in_specs=(
            P(("groups", "dp"), "adapter"),
            P(("groups", "dp"), "adapter"),
            P(("groups", "dp"), None),
            P("groups"),
            P(("groups", "adapter"), None, None),
            P(("groups", "adapter"), None, None),
        ),
        out_specs=(
            P(("groups", "dp"), "adapter"),
            P(("groups", "adapter"), None, None),
            P(("groups", "adapter"), None, None),
        ),
        check_vma=False,
    )
```

```python
import jax
import jax.numpy as jnp
from jax import lax
from jax.experimental import pallas as pl
from jax.experimental.pallas import tpu as pltpu
from jax.sharding import PartitionSpec as P

DKV = 1024
R = 64
BLOCK = 128
BF = jnp.bfloat16
F32 = jnp.float32
WHOLE = pl.BlockSpec(memory_space=pltpu.VMEM)
SCALARS = pl.BlockSpec(memory_space=pltpu.SMEM)
FAR = pl.BlockSpec(memory_space=pltpu.HBM)
EDGE, UPPER, ODD, PLACE, DP_PLACE = range(5)
(
    PART, FROM_LINE, OLD_PART, INNER, OLD_INNER, FROM_INNER, LINE, OLD_LINE, FINAL, FINALS,
    OLD_FINAL, WIDE, KEEP, SEND, SHRUNK_MINE, SHRUNK_THEIRS, KEPT, CAME, SLOT_ROWS,
    MARK,
) = range(20)


def launch(body, args, specs, outs, out_specs, scratch, mib, flops, moved, marks, grid=()):
    n_in, n_args, n_outs = len(args) + len(marks), len(args), len(outs)

    def kernel(*refs):
        refs[n_in + n_outs][...] = jnp.zeros((8, 128), F32)
        body(*refs[:n_args], *refs[n_in : n_in + n_outs], *refs[n_in + n_outs + 1 :])

    return pl.pallas_call(
        kernel,
        grid=grid,
        out_shape=[*outs, jax.ShapeDtypeStruct((8, 128), F32)],
        in_specs=[*specs, *[pl.BlockSpec(memory_space=pl.ANY)] * len(marks)],
        out_specs=[*out_specs, WHOLE],
        scratch_shapes=scratch,
        compiler_params=pltpu.CompilerParams(vmem_limit_bytes=mib * 1024 * 1024),
        cost_estimate=pl.CostEstimate(flops=flops, bytes_accessed=moved, transcendentals=0),
    )(*args, *marks)


def back_call(flags, slot_rows, up_stack, out_grad, marks, pieces=4):
    rows, cols = out_grad.shape
    wide = up_stack.shape[0]
    depth = rows // pieces

    def body(flag_ref, slot_ref, up_ref, grad_ref, out_ref, held, sems):
        copies = []
        for p in range(pieces):
            here = pl.ds(p * depth, depth)
            copies.append(pltpu.make_async_copy(grad_ref.at[here, :], held.at[p], sems.at[p]))
            copies[-1].start()
        for p in range(pieces):
            copies[p].wait()
            here = slice(p * depth, (p + 1) * depth)
            every = lax.dot_general(
                up_ref[...], held[p], (((1,), (1,)), ((), ())), preferred_element_type=F32
            )
            rel = jnp.bitwise_xor(slot_ref[:, here], flag_ref[PLACE])
            total = jnp.zeros((R, depth), F32)
            for m in range(wide // R):
                total += jnp.where(rel == m, every[m * R : (m + 1) * R], 0.0)
            out_ref[:, here] = total

    return launch(
        body,
        (flags, slot_rows, up_stack, out_grad),
        (SCALARS, WHOLE, WHOLE, FAR),
        (jax.ShapeDtypeStruct((R, rows), F32),),
        (WHOLE,),
        [pltpu.VMEM((pieces, depth, cols), BF), pltpu.SemaphoreType.DMA((pieces,))],
        8,
        2 * rows * cols * wide,
        rows * cols * 2,
        marks,
    )


def masked(slot, rank, count, lhs_ref):
    for m in range(count):
        lhs_ref[m * R : (m + 1) * R, :] = jnp.where(slot == m, rank, 0.0).astype(BF)


def tile_copies(wide_ref, held, sems, start):
    pieces, depth, width = held.shape
    copies = [
        pltpu.make_async_copy(
            wide_ref.at[pl.ds(p * depth, depth), pl.ds(start, width)], held.at[p], sems.at[p]
        )
        for p in range(pieces)
    ]
    for copy in copies:
        copy.start()
    return copies


def tile_dot(lhs_ref, held, copies):
    pieces, depth, width = held.shape
    total = jnp.zeros((lhs_ref.shape[0], width), F32)
    for p in range(pieces):
        copies[p].wait()
        total += jnp.dot(
            lhs_ref[:, p * depth : (p + 1) * depth], held[p], preferred_element_type=F32
        )
    return total.astype(BF)


def tile_scratch(rows, width, pieces=4):
    return [pltpu.VMEM((pieces, rows // pieces, width), BF), pltpu.SemaphoreType.DMA((pieces,))]


def first_call(flags, slot_rows, mine, theirs, acts, count, width, marks):
    rows = acts.shape[0]
    half = rows // 2

    def body(flag_ref, slot_ref, mine_ref, theirs_ref, acts_ref, out, lhs, d_own, d_half, held, sems):
        copies = tile_copies(acts_ref, held, sems, 0)
        rank = mine_ref[...] + theirs_ref[...]
        d_own[...] = rank.astype(BF)
        odd = flag_ref[ODD] == 1
        d_half[...] = jnp.where(odd, rank[:, half:], rank[:, :half]).astype(BF)
        masked(slot_ref[...], rank, count, lhs)
        out[...] = tile_dot(lhs, held, copies)

    return launch(
        body,
        (flags, slot_rows, mine, theirs, acts),
        (SCALARS, WHOLE, WHOLE, WHOLE, FAR),
        [
            jax.ShapeDtypeStruct((count * R, width), BF),
            jax.ShapeDtypeStruct((count * R, rows), BF),
            jax.ShapeDtypeStruct((R, rows), BF),
            jax.ShapeDtypeStruct((R, half), BF),
        ],
        [WHOLE] * 4,
        tile_scratch(rows, width),
        10,
        2 * rows * count * R * width,
        rows * width * 2,
        marks,
    )


def other_call(flags, slot_rows, mine, theirs, acts, tiles, count, marks):
    rows = acts.shape[0]
    n = len(tiles)
    total = sum(width for _, width in tiles)

    def body(flag_ref, slot_ref, mine_ref, theirs_ref, acts_ref, *refs):
        rank_ref, lhs = refs[n], refs[n + 1]
        held, sems = refs[n + 2 :: 2], refs[n + 3 :: 2]
        copies = [
            tile_copies(acts_ref, held[i], sems[i], start) for i, (start, _) in enumerate(tiles)
        ]
        odd = flag_ref[ODD] == 1
        a, b = mine_ref[...].astype(F32), theirs_ref[...].astype(F32)
        rank = jnp.concatenate([jnp.where(odd, b, a), jnp.where(odd, a, b)], axis=1)
        rank_ref[...] = rank.astype(BF)
        masked(slot_ref[...], rank, count, lhs)
        for i in range(n):
            refs[i][...] = tile_dot(lhs, held[i], copies[i])

    return launch(
        body,
        (flags, slot_rows, mine, theirs, acts),
        (SCALARS, WHOLE, WHOLE, WHOLE, FAR),
        [jax.ShapeDtypeStruct((count * R, width), BF) for _, width in tiles]
        + [jax.ShapeDtypeStruct((R, rows), BF)],
        [WHOLE] * (n + 1),
        [pltpu.VMEM((count * R, rows), BF)]
        + [x for _, width in tiles for x in tile_scratch(rows, width)],
        16,
        2 * rows * count * R * total,
        rows * total * 2,
        marks,
    )


def tiles_call(lhs, acts, tiles, marks):
    rows = acts.shape[0]
    n = len(tiles)
    total = sum(width for _, width in tiles)

    def body(lhs_ref, acts_ref, *refs):
        held, sems = refs[n::2], refs[n + 1 :: 2]
        copies = [
            tile_copies(acts_ref, held[i], sems[i], start) for i, (start, _) in enumerate(tiles)
        ]
        for i in range(n):
            refs[i][...] = tile_dot(lhs_ref, held[i], copies[i])

    return launch(
        body,
        (lhs, acts),
        (WHOLE, FAR),
        [jax.ShapeDtypeStruct((lhs.shape[0], width), BF) for _, width in tiles],
        [WHOLE] * n,
        [x for _, width in tiles for x in tile_scratch(rows, width)],
        12,
        2 * rows * lhs.shape[0] * total,
        rows * total * 2,
        marks,
    )


def place_call(position, firsts, seconds, start, total_rows, held):
    width = sum(part[2] for part in firsts)
    count = len(seconds[0][0])
    flat, reads = [], []
    for parts in (firsts, seconds):
        reads.append([])
        for arrays, offset, wide in parts:
            listed = isinstance(arrays, list)
            reads[-1].append((len(flat), listed, offset, wide))
            flat += arrays if listed else [arrays]
    extra = [] if held is None else [held]

    def kernel(flag_ref, *refs):
        out_ref, turned, sems = refs[-3:]

        def read(parts, m, here):
            got = []
            for k, listed, offset, wide in parts:
                cols = slice(offset, offset + wide)
                got.append(refs[k + m][:, cols] if listed else refs[k][here, cols])
            return jnp.concatenate(got, axis=1).astype(F32)

        copies = []
        for m in range(count):
            sender = jnp.bitwise_xor(flag_ref[PLACE], m)
            swapped = sender >= count // 2
            here = pl.ds(pl.multiple_of(sender * R, R), R)
            a, b = read(reads[0], m, here), read(reads[1], m, here)
            turned[m, :, :] = jnp.concatenate(
                [jnp.where(swapped, b, a), jnp.where(swapped, a, b)], axis=0
            ).T.astype(BF)
            row = pl.multiple_of(sender * (total_rows // count) + start, 128)
            copies.append(
                pltpu.make_async_copy(
                    turned.at[m], out_ref.at[pl.ds(row, width), :], sems.at[m]
                )
            )
            copies[-1].start()
        for copy in copies:
            copy.wait()

    return pl.pallas_call(
        kernel,
        out_shape=jax.ShapeDtypeStruct((total_rows, 2 * R), BF),
        in_specs=[SCALARS]
        + [WHOLE] * len(flat)
        + [pl.BlockSpec(memory_space=pl.ANY)] * len(extra),
        out_specs=pl.BlockSpec(memory_space=pl.ANY),
        scratch_shapes=[
            pltpu.VMEM((count, width, 2 * R), BF),
            pltpu.SemaphoreType.DMA((count,)),
        ],
        input_output_aliases={} if held is None else {1 + len(flat): 0},
        compiler_params=pltpu.CompilerParams(vmem_limit_bytes=12 * 1024 * 1024),
        cost_estimate=pl.CostEstimate(
            flops=15 * 10**9, bytes_accessed=4 * count * width * 2 * R * 2, transcendentals=0
        ),
    )(position, *flat, *extra)


def fold_call(pieces, groups, rows, marks):
    width = pieces.shape[1]
    per = pieces.shape[0] // groups // rows

    def body(in_ref, out_ref):
        for a in range(groups):
            total = jnp.zeros((rows, width), F32)
            for z in range(per):
                start = (a * per + z) * rows
                total += in_ref[start : start + rows, :].astype(F32)
            out_ref[:, a * width : (a + 1) * width] = total.astype(BF)

    return launch(
        body,
        (pieces,),
        (WHOLE,),
        [jax.ShapeDtypeStruct((rows, groups * width), BF)],
        [WHOLE],
        [],
        6,
        1,
        pieces.size * 3,
        marks,
    )[0]


def stack_call(flags, parts):
    rows, width = parts[0].shape

    def body(flag_ref, *refs):
        for m in range(len(parts)):
            place = jnp.bitwise_xor(flag_ref[DP_PLACE], m)
            refs[-1][pl.ds(pl.multiple_of(place * rows, rows), rows), :] = refs[m][...]

    return launch(
        body,
        (flags, *parts),
        (SCALARS, *[WHOLE] * len(parts)),
        [jax.ShapeDtypeStruct((rows * len(parts), width), BF)],
        [WHOLE],
        [],
        6,
        1,
        rows * width * 16,
        [],
    )[0]


def step_call(flags, arrays, outs, marks, count, start=None):
    names = list(arrays)
    out_names = list(outs)
    rows = None
    scratch = []
    mib = 4
    if start is not None:
        wide = arrays[WIDE]
        rows = wide.shape[0]
        width = outs[PART][1]
        scratch += tile_scratch(rows, width)
        scratch.append(pltpu.VMEM((count * R, rows), BF))
        mib += 7

    def body(flag_ref, *refs):
        got = dict(zip(names, refs[: len(names)]))
        put = dict(zip(out_names, refs[len(names) :]))
        rest = list(refs[len(names) + len(out_names) :])
        edge = flag_ref[EDGE] == 1
        inside = jnp.logical_not(edge)

        def add(a, b):
            return (got[a][...].astype(F32) + got[b][...].astype(F32)).astype(BF)

        if start is not None:
            held, sems = rest[:2]
            rest = rest[2:]
            copies = tile_copies(got[WIDE], held, sems, start)
        if INNER in put:
            put[INNER][...] = add(OLD_PART, FROM_LINE)
        if FINAL in put or (FINAL, 0) in put or FINALS in put:

            def finish(src):
                if FINAL in put:
                    put[FINAL][...] = src[...]
                elif FINALS in put:
                    first_width = got[OLD_FINAL].shape[1]
                    put[FINALS][:, :first_width] = got[OLD_FINAL][...]
                    put[FINALS][:, first_width:] = src[...]
                else:
                    for m in range(count):
                        place = jnp.bitwise_xor(flag_ref[PLACE], m)
                        here = pl.ds(pl.multiple_of(place * R, R), R)
                        first_width = 0
                        if OLD_FINAL in got:
                            first_width = got[OLD_FINAL].shape[1]
                            put[(FINAL, m)][:, :first_width] = got[OLD_FINAL][here, :]
                        put[(FINAL, m)][:, first_width:] = src[here, :]

            pl.when(edge)(lambda: finish(got[FROM_LINE]))
            pl.when(inside)(lambda: finish(got[OLD_LINE]))
        if KEEP in put:
            upper = flag_ref[UPPER] == 1
            key = got[SHRUNK_MINE][:R] + got[SHRUNK_THEIRS][:R]
            value = got[SHRUNK_MINE][R:] + got[SHRUNK_THEIRS][R:]
            put[KEEP][...] = jnp.where(upper, value, key)
            put[SEND][...] = jnp.where(upper, key, value).astype(BF)
        if start is not None:
            lhs = rest[0]
            rank = got[KEPT][...] + got[CAME][...].astype(F32)
            masked(got[SLOT_ROWS][...], rank, count, lhs)
            put[PART][...] = tile_dot(lhs, held, copies)
        if LINE in put:
            if OLD_INNER in got and PART in got:

                @pl.when(edge)
                def _():
                    put[LINE][...] = got[PART][...]

                @pl.when(inside)
                def _():
                    put[LINE][...] = add(OLD_INNER, FROM_INNER)

            elif OLD_INNER in got:
                put[LINE][...] = add(OLD_INNER, FROM_INNER)
            else:
                put[LINE][...] = got[PART][...]
    made = launch(
        body,
        (flags, *arrays.values()),
        (SCALARS, *[FAR if k == WIDE else WHOLE for k in names]),
        [
            jax.ShapeDtypeStruct(shape, F32 if k == KEEP else BF)
            for k, shape in outs.items()
        ],
        [WHOLE] * len(outs),
        scratch,
        mib,
        15 * 10**9 if FROM_LINE in names else 1,
        24 * 10**6,
        marks,
    )
    return dict(zip([*out_names, MARK], made))


def shrink_call(slot, pool, acts, marks, per=8):
    rows, width = acts.shape

    def body(slot_ref, pool_ref, acts_ref, out_ref):
        i = pl.program_id(0)
        for b in range(per):
            here = slice(b * BLOCK, (b + 1) * BLOCK)
            part = jnp.dot(
                acts_ref[here, :], pool_ref[slot_ref[i * per + b]], preferred_element_type=F32
            )
            out_ref[:, here] = part.T

    return launch(
        body,
        (slot, pool, acts),
        (SCALARS, WHOLE, pl.BlockSpec((per * BLOCK, width), lambda i: (i, 0))),
        (jax.ShapeDtypeStruct((2 * R, rows), F32),),
        (pl.BlockSpec((2 * R, per * BLOCK), lambda i: (0, i)),),
        [],
        16,
        4 * rows * width * 2 * R,
        rows * width * 2,
        marks,
        (rows // (BLOCK * per),),
    )


def expand_call(flags, slot, pools, own, other, width, marks, per=4):
    rows = own.shape[1]

    def body(flag_ref, slot_ref, *refs):
        pool_refs = refs[: len(pools)]
        own_ref, other_ref, out_ref = refs[len(pools) :]
        i = pl.program_id(0)
        upper = flag_ref[UPPER] == 1
        for b in range(per):
            here = slice(b * BLOCK, (b + 1) * BLOCK)
            mine, theirs = own_ref[:, here].astype(F32), other_ref[:, here].astype(F32)
            rank = jnp.concatenate(
                [jnp.where(upper, theirs, mine), jnp.where(upper, mine, theirs)], axis=0
            )
            turned = rank.T.astype(BF)
            first = 0
            for pool_ref in pool_refs:
                depth = pool_ref.shape[1]
                out_ref[here, first : first + depth] = lax.dot_general(
                    turned,
                    pool_ref[slot_ref[i * per + b]],
                    (((1,), (1,)), ((), ())),
                    preferred_element_type=F32,
                ).astype(BF)
                first += depth

    return launch(
        body,
        (flags, slot, *pools, own, other),
        (
            SCALARS,
            SCALARS,
            *[WHOLE] * len(pools),
            pl.BlockSpec((R, per * BLOCK), lambda i: (0, i)),
            pl.BlockSpec((R, per * BLOCK), lambda i: (0, i)),
        ),
        (pltpu.HBM((rows, width), BF),),
        (pl.BlockSpec((per * BLOCK, width), lambda i: (i, 0)),),
        [],
        12,
        4 * rows * width * 2 * R,
        rows * width * 2,
        marks,
        (rows // (BLOCK * per),),
    )


def local(acts, out_grad, tenant_ids, slot_map, down_pool, up_pool):
    acts = pltpu.with_memory_space_constraint(acts, pltpu.HBM)
    out_grad = pltpu.with_memory_space_constraint(out_grad, pltpu.HBM)
    count = lax.axis_size("adapter")
    j = lax.axis_index("adapter")
    z = lax.axis_index("dp")
    rows, width = acts.shape
    cols = out_grad.shape[1]
    total_rows = down_pool.shape[1]
    edge = (z == 0) | (z == 3)
    flags = jnp.stack([edge.astype(jnp.int32), j // (count // 2), j % 2, j, z]).astype(jnp.int32)

    def swap(x, m):
        return lax.ppermute(x, "adapter", [(i, i ^ m) for i in range(count)])

    def to_owner(x):
        return lax.all_to_all(x, "adapter", split_axis=0, concat_axis=0, tiled=True)

    slot = slot_map[tenant_ids[:, 0]].astype(jnp.int32)
    slot_rows = jnp.repeat(slot, BLOCK)[None, :]

    def up_piece(m):
        return lax.dynamic_slice(up_pool[0], (0, (j ^ m) * cols), (R, cols))

    ups = [up_piece(0)] + [swap(up_piece(m), m) for m in range(1, count)]
    back_part, mark = back_call(flags, slot_rows, jnp.concatenate(ups, axis=0), out_grad, [])
    back_peer = swap(back_part, 1)

    unit = width // 16
    sizes = [k * unit for k in (6, 5, 5, 5, 6, 5)]
    n = len(sizes)
    per_kind = n // 2
    starts = [sum(sizes[:c]) % width for c in range(n)]
    tenants = count * R
    parts, line, inner, from_line, from_inner, final = {}, {}, {}, {}, {}, {}
    parts[0], lhs_own, d_own, d_half, mark = first_call(
        flags, slot_rows, back_part, back_peer, acts, count, sizes[0], []
    )
    came_half = swap(d_half, 2)
    came_other = swap(came_half, 1)
    tiles = [(starts[c], sizes[c]) for c in range(1, per_kind)]
    *more, mark = tiles_call(lhs_own, acts, tiles, [mark])
    for c in range(1, per_kind):
        parts[c] = more[c - 1]
    pool_in, _, _ = lax.optimization_barrier((down_pool[0], mark, came_half))
    pool = to_owner(pool_in).reshape(count, width, 2 * R)
    pools = [pltpu.with_memory_space_constraint(pool, pltpu.HBM)]

    for t in range(n + 6):
        if t in (per_kind, per_kind + 1):
            which = range(t, t + 1) if t == per_kind else range(t, n)
            *more, d_other, mark = other_call(
                flags, slot_rows, came_half, came_other, acts,
                [(starts[c], sizes[c]) for c in which], count, [mark],
            )
            parts.update(zip(which, more))
        if t < 2:
            line[t] = parts[t]
        else:
            arrays, outs, start = {}, {}, None
            if t < n and t in parts:
                arrays[PART] = parts[t]
            arrays[FROM_LINE] = from_line[t - 2]
            if t - 2 < n:
                arrays[OLD_PART] = parts[t - 2]
                outs[INNER] = (tenants, sizes[t - 2])
            if 0 <= t - 4 < n:
                arrays[OLD_INNER] = inner[t - 2]
                arrays[FROM_INNER] = from_inner[t - 2]
            if t < n or 0 <= t - 4 < n:
                outs[LINE] = (tenants, sizes[t] if t < n else sizes[t - 4])
            if t >= 6:
                arrays[OLD_LINE] = line[t - 2]
                c = t - 6
                if c in (0, per_kind - 1, n - 2):
                    outs[FINAL] = (tenants, sizes[c])
                else:
                    arrays[OLD_FINAL] = final[c - 1]
                    wide_now = final[c - 1].shape[1] + sizes[c]
                    if c >= per_kind:
                        outs.update({(FINAL, m): (R, wide_now) for m in range(count)})
                    else:
                        outs[FINALS] = (tenants, wide_now)
            if t == 8:
                arrays[SHRUNK_MINE], arrays[SHRUNK_THEIRS] = shrunk_part, swap(shrunk_part, 1)
                outs[KEEP] = outs[SEND] = (R, rows)
            marks = [mark]
            if t == 10:
                late = {WIDE: out_grad, KEPT: keep, CAME: came_shrunk, SLOT_ROWS: slot_rows}
                made = step_call(flags, late, {PART: (tenants, cols)}, [mark], count, 0)
                up, mark = made[PART], made[MARK]
                marks = [mark, own]
                up_pieces = lax.all_to_all(
                    up, ("adapter", "dp"), split_axis=0, concat_axis=0, tiled=True
                )
            if t == 9:
                acts_grad, mark = expand_call(flags, slot, pools, d_own, d_other, width, [mark])
                marks = [mark]
            if t == 6:
                shrunk_part, mark = shrink_call(slot, pools[0], acts, [mark])
                marks = [mark]
            made = step_call(flags, arrays, outs, marks, count, start)
            mark = made[MARK]
            if PART in made and t < n:
                parts[t] = made[PART]
            if INNER in made:
                inner[t] = made[INNER]
            if LINE in made:
                line[t] = made[LINE]
            if FINAL in made:
                final[t - 6] = made[FINAL]
            if FINALS in made:
                final[t - 6] = made[FINALS]
            if t == 7:
                own = to_owner(made[FINALS])
            if (FINAL, 0) in made:
                final[t - 6] = [made[(FINAL, 0)]] + [
                    swap(made[(FINAL, m)], m) for m in range(1, count)
                ]
            if t == 8:
                keep, came_shrunk = made[KEEP], swap(made[SEND], 2)
        if t in line and t < n + 4:
            from_line[t] = lax.ppermute(line[t], "dp", [(0, 1), (1, 0), (2, 3), (3, 2)])
        if t in inner:
            from_inner[t] = lax.ppermute(inner[t], "dp", [(1, 2), (2, 1)])

    dp = lax.axis_size("dp")
    up_rows = fold_call(up_pieces, count, R // dp, [mark])
    up_parts = [up_rows] + [
        lax.ppermute(up_rows, "dp", [(i, i ^ m) for i in range(dp)]) for m in range(1, dp)
    ]
    up_grad = stack_call(flags, up_parts)
    down_grad = None
    mixed, last = final[per_kind], final[n - 1]
    joint, split = sizes[0] + sizes[1], sizes[per_kind]
    down_grad = place_call(
        flags, [(own, 0, split)], [(mixed, width - joint, split)], 0, total_rows, None
    )
    down_grad = place_call(
        flags,
        [(own, split, joint - split), (mixed, 0, width - joint)],
        [(last, 0, width - split)],
        split,
        total_rows,
        down_grad,
    )
    return acts_grad, down_grad[None], up_grad[None]


def local_any(acts, out_grad, tenant_ids, slot_map, down_pool, up_pool):
    position = lax.axis_index("adapter")
    row_count, local_width = acts.shape
    col_count = out_grad.shape[1]
    block_count = row_count // BLOCK
    tenant_slot = slot_map[tenant_ids[:, 0]]
    down_slices = lax.all_to_all(down_pool, "adapter", split_axis=1, concat_axis=0, tiled=True)
    up_slices = lax.all_to_all(up_pool, "adapter", split_axis=2, concat_axis=0, tiled=True)
    tenant_count = down_slices.shape[0]
    acts_blocks = acts.reshape(block_count, BLOCK, local_width)
    grad_blocks = out_grad.reshape(block_count, BLOCK, col_count)
    down_blocks = down_slices[tenant_slot]
    up_blocks = up_slices[tenant_slot]
    shrunk_part = jnp.einsum(
        "bnd,bdr->bnr", acts_blocks, down_blocks, preferred_element_type=jnp.float32
    )
    back_part = jnp.einsum(
        "bnc,brc->bnr", grad_blocks, up_blocks, preferred_element_type=jnp.float32
    )
    is_key = position * col_count < DKV
    zero_part = jnp.zeros_like(back_part)
    d_part = jnp.where(
        is_key,
        jnp.concatenate([back_part, zero_part], axis=-1),
        jnp.concatenate([zero_part, back_part], axis=-1),
    )
    shrunk_sum, d_sum = lax.psum((shrunk_part, d_part), "adapter")
    shrunk = shrunk_sum.astype(jnp.bfloat16)
    d_shrunk = d_sum.astype(jnp.bfloat16)
    acts_grad = jnp.einsum(
        "bnr,bdr->bnd", d_shrunk, down_blocks, preferred_element_type=jnp.float32
    )
    acts_grad = acts_grad.astype(jnp.bfloat16).reshape(row_count, local_width)
    part_down = jnp.einsum(
        "bnd,bnr->bdr", acts_blocks, d_shrunk, preferred_element_type=jnp.float32
    )
    own_shrunk = jnp.where(is_key, shrunk[..., :R], shrunk[..., R:])
    part_up = jnp.einsum(
        "bnr,bnc->brc", own_shrunk, grad_blocks, preferred_element_type=jnp.float32
    )
    member = (tenant_slot[None, :] == jnp.arange(tenant_count, dtype=jnp.int32)[:, None]).astype(
        jnp.float32
    )
    grad_down = jnp.einsum("tb,bdr->tdr", member, part_down, precision=lax.Precision.HIGHEST)
    grad_up = jnp.einsum("tb,brc->trc", member, part_up, precision=lax.Precision.HIGHEST)
    owned_down = lax.all_to_all(grad_down, "adapter", split_axis=0, concat_axis=1, tiled=True)
    owned_up = lax.all_to_all(grad_up, "adapter", split_axis=0, concat_axis=2, tiled=True)
    total_down, total_up = lax.psum((owned_down, owned_up), "dp")
    down_grad = total_down.astype(jnp.bfloat16)
    up_grad = total_up.astype(jnp.bfloat16)
    return (acts_grad, down_grad, up_grad)


def solution(mesh):
    line_of_four = mesh.shape["adapter"] == 4 and mesh.shape["dp"] == 4
    return jax.shard_map(
        local if line_of_four else local_any,
        mesh=mesh,
        in_specs=(
            P(("groups", "dp"), "adapter"),
            P(("groups", "dp"), "adapter"),
            P(("groups", "dp"), None),
            P("groups"),
            P(("groups", "adapter"), None, None),
            P(("groups", "adapter"), None, None),
        ),
        out_specs=(
            P(("groups", "dp"), "adapter"),
            P(("groups", "adapter"), None, None),
            P(("groups", "adapter"), None, None),
        ),
        check_vma=False,
    )
```
